32 devices in a mesh: seq: 2 (over y), fsdp: 16 (over z, x, core).
Axes of the slice: x: 2, y: 2, z: 4, core: 2. Of those that a mesh axis runs over, the one named last changes fastest.
Arguments:
- tokens: bfloat16 [2, 16, 256, 1792], P(None, 'fsdp', 'seq'), may hold values from -6 to 6
- seq_order: int32 [2, 16, 2, 128], P(None, 'fsdp', 'seq'), may hold values from 0 to 127, each once within a row
- seq_lengths: int32 [2, 16, 4], P(None, 'fsdp'), may hold values from 1 to 253, as said below
- valid_count: int32 [2, 16], P(None, 'fsdp'), may hold values from 32 to 246, as said below
- teacher: bfloat16 [2, 16, 256, 1792], P(None, 'fsdp', 'seq'), may hold values from -6 to 6
- norm_one: bfloat16 [1792], P('fsdp'), may hold values from 0.099609375 to 1.8984375
- w_query: bfloat16 [1792, 256], P('fsdp'), may hold values from -0.125 to 0.125
- w_key: bfloat16 [1792, 256], P('fsdp'), may hold values from -0.125 to 0.125
- w_value: bfloat16 [1792, 1792], P('fsdp'), may hold values from -0.125 to 0.125
- conv_taps: bfloat16 [3, 1792], P(None, 'fsdp'), may hold values from -3 to 3
- w_out: bfloat16 [1792, 1792], P('fsdp'), may hold values from -2 to 2
- norm_two: bfloat16 [1792], P('fsdp'), may hold values from 0.099609375 to 1.8984375
- w_gate: bfloat16 [1792, 4864], P('fsdp'), may hold values from -0.125 to 0.125
- w_up: bfloat16 [1792, 4864], P('fsdp'), may hold values from -0.125 to 0.125
- w_down: bfloat16 [4864, 1792], P('fsdp'), may hold values from -0.078125 to 0.078125
Outputs:
- output: bfloat16 [2, 16, 256, 1792], P(None, 'fsdp', 'seq')
- input_grad: bfloat16 [2, 16, 256, 1792], P(None, 'fsdp', 'seq')
- grad_norm_one: float32 [1792], P('fsdp')
- grad_w_query: float32 [1792, 256], P('fsdp')
- grad_w_key: float32 [1792, 256], P('fsdp')
- grad_w_value: float32 [1792, 1792], P('fsdp')
- grad_conv_taps: float32 [3, 1792], P(None, 'fsdp')
- grad_w_out: float32 [1792, 1792], P('fsdp')
- grad_norm_two: float32 [1792], P('fsdp')
- grad_w_gate: float32 [1792, 4864], P('fsdp')
- grad_w_up: float32 [1792, 4864], P('fsdp')
- grad_w_down: float32 [4864, 1792], P('fsdp')
- loss: float32 [], replicated
The draws below stay inside these ranges and needn't reach their ends.
Inputs may be any that keep to these rules, and one draw needn't show every extreme that they name: `seq_lengths`: in each micro-batch and group the 4 lengths are positive and sum to 256; all but one of them are at most 10. `valid_count`: the loss counts, in each micro-batch and group, the tokens whose given position in the group is below this count. `seq_order`: each row of 128 entries is a permutation.
All inputs are finite; a program needn't handle non-finite values.
Results may differ from the reference program's by a relative error of at most 0.015.
Values may be sent and summed in bfloat16 or wider, within the bound.
No kernel may reach another device: no remote copies, remote signals or barrier semaphores. Data moves between devices by JAX's collectives and lax.ppermute only.
A program may use at most 384 MiB of HBM per device.

```python
import jax
import jax.numpy as jnp
from jax import lax

D = 1792
FF = 4864
HEADS = 16
FEAT = 16
TAPS = 3
NSEG = 4
SHORT_MOST = 10
MB = 2
TOK_DEV = 128
HEAD_SIZE = 112
QK = 256
SEQ_DEVS = 2
GROUPS = 16
GROUP_TOK = 256


def draw_seq_lengths(key, part):
    key = jax.random.fold_in(key, 11)
    short_key, place_key = jax.random.split(key)
    shorts = jax.random.randint(short_key, (MB, GROUPS, NSEG), 1, SHORT_MOST + 1)
    first_group = (jnp.arange(MB, dtype=jnp.int32)[:, None, None] == 0) & (jnp.arange(GROUPS, dtype=jnp.int32)[None, :, None] == 0)
    shorts = jnp.where(first_group, 1, shorts)
    long_slot = jax.random.randint(place_key, (MB, GROUPS, 1), 0, NSEG)
    chosen = jnp.arange(NSEG, dtype=jnp.int32)[None, None, :] == long_slot
    others = jnp.sum(jnp.where(chosen, 0, shorts), axis=2, keepdims=True)
    return jnp.where(chosen, GROUP_TOK - others, shorts).astype(jnp.int32)


def draw_valid_count(key, part):
    key = jax.random.fold_in(key, 23)
    rising = GROUP_TOK // 8 + jnp.arange(GROUPS, dtype=jnp.int32) * (GROUP_TOK * 5 // 8) // GROUPS
    jitter = jax.random.randint(key, (MB, GROUPS), 0, GROUP_TOK // 4 + 1)
    micro_first = jnp.arange(MB, dtype=jnp.int32)[:, None] == 0
    group_index = jnp.arange(GROUPS, dtype=jnp.int32)[None, :]
    jitter = jnp.where(micro_first & (group_index == 0), 0, jitter)
    jitter = jnp.where(micro_first & (group_index == GROUPS - 1), GROUP_TOK // 4, jitter)
    return (rising[None, :] + jitter).astype(jnp.int32)


def steps_of(rng, shape, cuts, least, top_value):
    def one(dim, blocks):
        heights = jax.random.uniform(jax.random.fold_in(jax.random.fold_in(rng, 6), dim), (blocks,), jnp.float32, least / len(cuts), top_value / len(cuts))
        return jnp.repeat(jnp.exp(heights), shape[dim] // blocks).reshape((-1,) + (1,) * (len(shape) - dim - 1))

    factor_of = one(*cuts[0])
    for cut in cuts[1:]:
        factor_of = factor_of * one(*cut)
    return factor_of


def centred(stream_key, shape, spread, bound, pieces=(), kind=jnp.bfloat16):
    factor_of = steps_of(stream_key, shape, pieces, -0.22, 0.18) if pieces else 1.0
    values = jax.random.normal(stream_key, shape, jnp.float32) * spread * factor_of
    return jnp.minimum(jnp.maximum(values, -bound), bound).astype(kind)


def setup_inputs(seed: int = 0) -> dict:
    keys = jax.random.split(jax.random.key(seed), 16)
    return {
        "tokens": centred(keys[0], (MB, GROUPS, GROUP_TOK, D), 1.0, 6.0, ((1, 16), (2, 2))),
        "seq_order": jax.vmap(lambda own: jax.random.permutation(own, TOK_DEV))(jax.random.split(keys[1], MB * GROUPS * SEQ_DEVS)).reshape((MB, GROUPS, SEQ_DEVS, TOK_DEV)).astype(jnp.int32),
        "seq_lengths": draw_seq_lengths(jax.random.fold_in(keys[15], 71), 0),
        "valid_count": draw_valid_count(jax.random.fold_in(keys[15], 71), 0),
        "teacher": centred(keys[4], (MB, GROUPS, GROUP_TOK, D), 1.0, 6.0, ((1, 16), (2, 2))),
        "norm_one": jnp.clip(1.0 + 0.18 * jax.random.normal(keys[5], (D,), jnp.float32), 0.099609375, 1.8984375).astype(jnp.bfloat16),
        "w_query": centred(keys[6], (D, QK), D ** -0.5, 0.125, ((0, 16),)),
        "w_key": centred(keys[7], (D, QK), D ** -0.5, 0.125, ((0, 16),)),
        "w_value": centred(keys[8], (D, D), D ** -0.5, 0.125, ((0, 16),)),
        "conv_taps": centred(keys[9], (TAPS, D), 0.5, 3.0, ((1, 16),)),
        "w_out": centred(keys[10], (D, D), (max(D // 256, 1)) ** -0.5, 2.0, ((0, 16),)),
        "norm_two": jnp.clip(1.0 + 0.18 * jax.random.normal(keys[11], (D,), jnp.float32), 0.099609375, 1.8984375).astype(jnp.bfloat16),
        "w_gate": centred(keys[12], (D, FF), D ** -0.5, 0.125, ((0, 16),)),
        "w_up": centred(keys[13], (D, FF), D ** -0.5, 0.125, ((0, 16),)),
        "w_down": centred(keys[14], (FF, D), FF ** -0.5, 0.078125, ((0, 16),)),
    }


@jax.custom_vjp
def low(v):
    return lax.optimization_barrier(v.astype(jnp.bfloat16)).astype(jnp.float32)

@jax.custom_vjp
def low_back(v):
    return v

def low_keep(v):
    return (low(v), None)

def low_pass(kept, grad):
    return (grad,)

def back_keep(v):
    return (v, None)

def back_low(kept, grad):
    return (low(grad),)
low.defvjp(low_keep, low_pass)
low_back.defvjp(back_keep, back_low)
HIGHEST = lax.Precision.HIGHEST
EPSILON = 1e-05

def matmul_high(left, right):
    return jnp.dot(left, right, precision=HIGHEST, preferred_element_type=jnp.float32)

def rms_norm(values, gain):
    return values * lax.rsqrt(lax.optimization_barrier(jnp.mean(values * values, axis=-1, keepdims=True)) + EPSILON) * gain

def segment_ids(lengths, positions):
    seq_ends = jnp.cumsum(lengths)
    return lax.optimization_barrier(jnp.sum((positions[:, None] >= seq_ends[None, :]).astype(jnp.int32), axis=1))

def layer_group(inputs, targets, order_rows, lengths, valid_rows, weights):
    norm_one, w_query, w_key, w_value, conv_taps, w_out, norm_two, w_gate, w_up, w_down = weights
    offsets = jnp.arange(SEQ_DEVS, dtype=jnp.int32)[:, None] * TOK_DEV
    gather_idx = (order_rows.astype(jnp.int32) + offsets).reshape(GROUP_TOK)
    positions = jnp.arange(GROUP_TOK, dtype=jnp.int32)
    inverse = jnp.zeros((GROUP_TOK,), jnp.int32).at[gather_idx].set(positions)
    packed = inputs[gather_idx]
    segment = segment_ids(lengths, positions)
    normed_one = low(rms_norm(packed, norm_one))
    queries = low_back(low(matmul_high(normed_one, w_query))).reshape(GROUP_TOK, HEADS, FEAT)
    keys_rows = low_back(low(matmul_high(normed_one, w_key))).reshape(GROUP_TOK, HEADS, FEAT)
    values = low_back(low(matmul_high(normed_one, w_value)))
    value_heads = values.reshape(GROUP_TOK, HEADS, HEAD_SIZE)
    scores = jnp.einsum('thf,uhf->htu', queries, keys_rows, precision=HIGHEST) * 0.25
    allowed = ((segment[:, None] == segment[None, :]) & (positions[:, None] >= positions[None, :])).astype(jnp.float32)
    kernel = (1.0 + scores + 0.5 * scores * scores) * allowed[None]
    numerator = jnp.einsum('htu,uhe->the', kernel, value_heads, precision=HIGHEST)
    denominator = jnp.transpose(lax.optimization_barrier(jnp.sum(kernel, axis=2)))
    attended = (numerator / denominator[:, :, None]).reshape(GROUP_TOK, D)
    same_one = (segment[1:] == segment[:-1]).astype(jnp.float32)
    same_two = (segment[2:] == segment[:-2]).astype(jnp.float32)
    prev_one = jnp.concatenate([jnp.zeros((1, D), jnp.float32), values[:-1] * same_one[:, None]], axis=0)
    prev_two = jnp.concatenate([jnp.zeros((2, D), jnp.float32), values[:-2] * same_two[:, None]], axis=0)
    conv_out = conv_taps[0] * values + conv_taps[1] * prev_one + conv_taps[2] * prev_two
    mixed_rows = low(attended * jax.nn.silu(conv_out))
    residual = packed + low_back(matmul_high(mixed_rows, w_out))
    normed_two = low(rms_norm(residual, norm_two))
    gate_proj = low_back(matmul_high(normed_two, w_gate))
    up_proj = low_back(matmul_high(normed_two, w_up))
    hidden = low(jax.nn.silu(gate_proj) * up_proj)
    result = (residual + low_back(matmul_high(hidden, w_down)))[inverse]
    keep_mask = (positions < valid_rows).astype(jnp.float32)
    deviation = (result - targets) * keep_mask[:, None]
    return (result, jnp.sum(deviation * deviation))

def reference(tokens, seq_order, seq_lengths, valid_count, teacher, norm_one, w_query, w_key, w_value, conv_taps, w_out, norm_two, w_gate, w_up, w_down):
    weights = tuple((weight_item.astype(jnp.float32) for weight_item in (norm_one, w_query, w_key, w_value, conv_taps, w_out, norm_two, w_gate, w_up, w_down)))
    inputs = tokens.astype(jnp.float32).reshape(MB * GROUPS, GROUP_TOK, D)
    targets = teacher.astype(jnp.float32).reshape(MB * GROUPS, GROUP_TOK, D)
    orders = seq_order.reshape(MB * GROUPS, SEQ_DEVS, TOK_DEV)
    lengths = seq_lengths.reshape(MB * GROUPS, NSEG)
    valids = valid_count.reshape(MB * GROUPS)
    counted = jnp.sum(valid_count).astype(jnp.float32)
    slots = 0.5 * MB * GROUPS * GROUP_TOK

    def forward(inputs, weights):

        def one_group(packet):
            return jax.checkpoint(layer_group)(packet[0], packet[1], packet[2], packet[3], packet[4], weights)
        results, squares = lax.map(one_group, (inputs, targets, orders, lengths, valids))
        return (results, jnp.sum(squares) * slots / counted)
    (results, objective), pullback = jax.vjp(forward, inputs, weights)
    input_grad, grads = pullback((jnp.zeros_like(results), jnp.ones_like(objective)))
    loss = objective / (slots * D)
    output = results.reshape(MB, GROUPS, GROUP_TOK, D).astype(jnp.bfloat16)
    input_grad = input_grad.reshape(MB, GROUPS, GROUP_TOK, D).astype(jnp.bfloat16)
    return (output, input_grad, grads[0], grads[1], grads[2], grads[3], grads[4], grads[5], grads[6], grads[7], grads[8], grads[9], loss)
```

```python
from functools import partial

import jax
import jax.numpy as jnp
from jax import lax
from jax.experimental import pallas as pl
from jax.experimental.pallas import tpu as pltpu
from jax.sharding import PartitionSpec as P

HEADS = 16
FEAT = 16
HEAD_SIZE = 112
Z_CHIPS = 4
CORES = 2
SMALL = 128
EPSILON = 1e-05
BF16 = jnp.bfloat16
F32 = jnp.float32


def dot(left, right, dims=((1,), (0,))):
    return lax.dot_general(left, right, (dims, ((), ())), preferred_element_type=F32)


def take(array, index, axis):
    return lax.dynamic_index_in_dim(array, index, axis, keepdims=False)


class Place:
    def __init__(self):
        self.seqs = lax.axis_size("seq")
        self.fsdp = lax.axis_size("fsdp")
        self.xs = self.fsdp // (Z_CHIPS * CORES)
        self.y = lax.axis_index("seq")
        self.p = lax.axis_index("fsdp")
        self.c = self.p % CORES
        self.x = (self.p // CORES) % self.xs
        self.z = self.p // (CORES * self.xs)
        self.z_low_size = Z_CHIPS // self.seqs
        self.z_high = self.z // self.z_low_size

    def index(self, z, x, c):
        return (z * self.xs + x) * CORES + c

    def everyone(self):
        for z in range(Z_CHIPS):
            for x in range(self.xs):
                for c in range(CORES):
                    yield z, x, c


def seq_pieces(place, value):
    got = [value]
    for k in range(1, place.seqs):
        pairs = [(i, (i + k) % place.seqs) for i in range(place.seqs)]
        got.append(lax.ppermute(value, "seq", pairs))
    if place.seqs == 2:
        first = place.y == 0
        return [jnp.where(first, got[0], got[1]), jnp.where(first, got[1], got[0])]
    stacked = jnp.stack(got)
    return [take(stacked, (place.y - j) % place.seqs, 0) for j in range(place.seqs)]


def seq_scatter(place, value, axis):
    total = take(value, place.y, axis).astype(F32)
    for k in range(1, place.seqs):
        pairs = [(i, (i + k) % place.seqs) for i in range(place.seqs)]
        sent = take(value, (place.y + k) % place.seqs, axis).astype(BF16)
        total = total + lax.ppermute(sent, "seq", pairs).astype(F32)
    return total


def add_low(*parts):
    total = parts[0].astype(F32)
    for part in parts[1:]:
        total = total + part.astype(F32)
    return total.astype(BF16)


def line_scatter(value, axis, count, index, pairs_of):
    if count == 2:
        got = lax.ppermute(take(value, 1 - index, axis), "fsdp", pairs_of([(0, 1), (1, 0)]))
        return add_low(take(value, index, axis), got)
    up = down = None
    for far in range(count - 1, 0, -1):
        send_up = take(value, (index + far) % count, axis)
        send_down = take(value, (index - far) % count, axis)
        if up is not None:
            send_up = add_low(send_up, up)
            send_down = add_low(send_down, down)
        up = lax.ppermute(
            send_up, "fsdp", pairs_of([(i, i + 1) for i in range(count - far)])
        )
        down = lax.ppermute(
            send_down, "fsdp", pairs_of([(i, i - 1) for i in range(far, count)])
        )
    return add_low(take(value, index, axis), up, down)


def grad_scatter(place, grad):
    def core_pairs(moves):
        return [
            (place.index(z, x, a), place.index(z, x, b))
            for a, b in moves
            for z in range(Z_CHIPS)
            for x in range(place.xs)
        ]

    def x_pairs(moves):
        return [
            (place.index(z, a, c), place.index(z, b, c))
            for a, b in moves
            for z in range(Z_CHIPS)
            for c in range(CORES)
        ]

    def z_pairs(moves):
        return [
            (place.index(a, x, c), place.index(b, x, c))
            for a, b in moves
            for x in range(place.xs)
            for c in range(CORES)
        ]

    one_core = line_scatter(grad, 2, CORES, place.c, core_pairs)
    one_x = line_scatter(one_core, 1, place.xs, place.x, x_pairs)
    return line_scatter(one_x, 0, Z_CHIPS, place.z, z_pairs)


def plane_pairs(place, k):
    pairs = []
    for y in range(place.seqs):
        for z, x, c in place.everyone():
            high, low = divmod(z, place.z_low_size)
            if high == y:
                other = ((y + k) % place.seqs) * place.z_low_size + low
                pairs.append(
                    (
                        y * place.fsdp + place.index(z, x, c),
                        y * place.fsdp + place.index(other, x, c),
                    )
                )
    return pairs


def spread_rows(place, shard):
    rows = shard.shape[0] // place.seqs
    pieces = shard.reshape(place.seqs, rows, shard.shape[1])
    part = take(pieces, place.y, 0)
    owner = place.z_high == place.y
    for k in range(1, place.seqs):
        sent = take(pieces, (place.y + k) % place.seqs, 0)
        got = lax.ppermute(sent, ("seq", "fsdp"), plane_pairs(place, k))
        part = jnp.where((place.z_high - place.y) % place.seqs == k, got, part)
    return part


def plane_rows(place, gathered):
    rows, columns = gathered.shape
    blocks = gathered.reshape(place.seqs, place.fsdp // place.seqs, -1, columns)
    return jnp.swapaxes(blocks, 0, 1).reshape(rows, columns)


def plane_grad_view(place, grad):
    rows, columns = grad.shape
    view = grad.reshape(place.z_low_size, place.xs, CORES, place.seqs, -1, columns)
    view = jnp.transpose(view, (3, 0, 1, 2, 4, 5))
    return view.reshape(Z_CHIPS, place.xs, CORES, -1, columns)


def unspread_rows(place, part):
    seqs = place.seqs
    rows, columns = part.shape
    shard = jnp.zeros((seqs, rows, columns), part.dtype)
    shard = lax.dynamic_update_index_in_dim(shard, part, place.y, 0)
    for k in range(1, seqs):
        pairs = [(b, a) for a, b in plane_pairs(place, k)]
        got = lax.ppermute(part, ("seq", "fsdp"), pairs)
        shard = lax.dynamic_update_index_in_dim(shard, got, (place.y + k) % seqs, 0)
    shard = shard.reshape(seqs * rows, columns)
    whole = shard
    for k in range(1, seqs):
        pairs = []
        for y in range(seqs):
            for z, x, c in place.everyone():
                if z // place.z_low_size == y:
                    pairs.append(
                        (
                            y * place.fsdp + place.index(z, x, c),
                            ((y + k) % seqs) * place.fsdp + place.index(z, x, c),
                        )
                    )
        got = lax.ppermute(shard, ("seq", "fsdp"), pairs)
        whole = jnp.where((place.y - place.z_high) % seqs == k, got, whole)
    return whole.astype(F32)


def sum_everywhere(place, value):
    for axis, count in (("fsdp", place.fsdp), ("seq", place.seqs)):
        bit = 1
        while bit < count:
            value = value + lax.ppermute(value, axis, [(i, i ^ bit) for i in range(count)])
            bit *= 2
    return value


def head_window(head):
    low = head * HEAD_SIZE // 128 * 128
    high = -(-(head + 1) * HEAD_SIZE // 128) * 128
    return low, high


def sigmoid(value):
    return 1.0 / (1.0 + jnp.exp(-value))


def conv_parts(values, taps_ref, seg_col):
    rows = values.shape[0]
    index = lax.broadcasted_iota(jnp.int32, (rows, 1), 0)
    near_one = (index >= 1) & (pltpu.roll(seg_col, 1, 0) == seg_col)
    near_two = (index >= 2) & (pltpu.roll(seg_col, 2, 0) == seg_col)
    prev_one = jnp.where(near_one, pltpu.roll(values, 1, 0), 0.0)
    prev_two = jnp.where(near_two, pltpu.roll(values, 2, 0), 0.0)
    conv = taps_ref[0:1] * values + taps_ref[1:2] * prev_one + taps_ref[2:3] * prev_two
    return conv, prev_one, prev_two, near_one, near_two


def masks(rows, seg_col, seg_row):
    at = lax.broadcasted_iota(jnp.int32, (rows, rows), 0)
    of = lax.broadcasted_iota(jnp.int32, (rows, rows), 1)
    return (seg_col == seg_row) & (at >= of)


def lanes_between(low, high, start, stop):
    lane = low + lax.broadcasted_iota(jnp.int32, (1, high - low), 1)
    return (lane >= start) & (lane < stop)


def mix_kernel(heads, qkv_ref, taps_ref, segc_ref, segr_ref, mixed_ref, att_ref):
    rows = qkv_ref.shape[0]
    qk_width = heads * FEAT
    width = heads * HEAD_SIZE
    seg_col = segc_ref[0]
    allowed = masks(rows, seg_col, segr_ref[0])
    queries = qkv_ref[:, 0:qk_width]
    keys = qkv_ref[:, qk_width : 2 * qk_width]
    for head in range(heads):
        mine = lanes_between(0, qk_width, head * FEAT, (head + 1) * FEAT)
        query = jnp.where(mine, queries, jnp.zeros_like(queries))
        scores = dot(query, keys, ((1,), (1,))) * 0.25
        kern = jnp.where(allowed, 1.0 + scores + 0.5 * scores * scores, 0.0)
        den = jnp.sum(kern, axis=1, keepdims=True)
        low, high = head_window(head)
        high = min(high, width)
        num = dot(kern.astype(BF16), qkv_ref[:, 2 * qk_width + low : 2 * qk_width + high])
        here = lanes_between(low, high, head * HEAD_SIZE, (head + 1) * HEAD_SIZE)
        att_ref[:, low:high] = jnp.where(here, num * (1.0 / den), att_ref[:, low:high])
    values = qkv_ref[:, 2 * qk_width : 2 * qk_width + width].astype(F32)
    conv = conv_parts(values, taps_ref, seg_col)[0]
    mixed_ref[...] = (att_ref[...] * conv * sigmoid(conv)).astype(BF16)


def mix_back_kernel(
    heads, qkv_ref, dmixed_ref, taps_ref, segc_ref, segr_ref, dqkv_ref, dtaps_ref,
    att_ref, silu_ref, dv_ref,
):
    rows = qkv_ref.shape[0]
    qk_width = heads * FEAT
    width = heads * HEAD_SIZE
    seg_col = segc_ref[0]
    allowed = masks(rows, seg_col, segr_ref[0])
    queries = qkv_ref[:, 0:qk_width]
    keys = qkv_ref[:, qk_width : 2 * qk_width]
    values = qkv_ref[:, 2 * qk_width : 2 * qk_width + width].astype(F32)
    conv, prev_one, prev_two, near_one, near_two = conv_parts(values, taps_ref, seg_col)
    sig = sigmoid(conv)
    silu_ref[...] = dmixed_ref[...] * conv * sig
    dv_ref[...] = jnp.zeros_like(dv_ref)
    dq = jnp.zeros((rows, qk_width), F32)
    dk = jnp.zeros((rows, qk_width), F32)
    for head in range(heads):
        mine = lanes_between(0, qk_width, head * FEAT, (head + 1) * FEAT)
        query = jnp.where(mine, queries, jnp.zeros_like(queries))
        scores = dot(query, keys, ((1,), (1,))) * 0.25
        kern = jnp.where(allowed, 1.0 + scores + 0.5 * scores * scores, 0.0)
        inv_den = 1.0 / jnp.sum(kern, axis=1, keepdims=True)
        kern_low = kern.astype(BF16)
        low, high = head_window(head)
        high = min(high, width)
        value = qkv_ref[:, 2 * qk_width + low : 2 * qk_width + high]
        att = dot(kern_low, value) * inv_den
        here = lanes_between(low, high, head * HEAD_SIZE, (head + 1) * HEAD_SIZE)
        att_ref[:, low:high] = jnp.where(here, att, att_ref[:, low:high])
        datt = jnp.where(here, silu_ref[:, low:high], 0.0) * inv_den
        row_dot = jnp.sum(datt * att, axis=1, keepdims=True)
        datt_low = datt.astype(BF16)
        dkern = dot(datt_low, value, ((1,), (1,))) - row_dot
        dscores = jnp.where(allowed, dkern * (0.25 + 0.25 * scores), 0.0).astype(BF16)
        dq = dq + jnp.where(mine, dot(dscores, keys), 0.0)
        dk = dk + dot(dscores, query, ((0,), (0,)))
        dv_ref[:, low:high] += dot(kern_low, datt_low, ((0,), (0,)))
    dconv = dmixed_ref[...] * att_ref[...] * sig * (1.0 + conv * (1.0 - sig))
    dtaps_ref[0, 0:1] = jnp.sum(dconv * values, axis=0, keepdims=True)
    dtaps_ref[0, 1:2] = jnp.sum(dconv * prev_one, axis=0, keepdims=True)
    dtaps_ref[0, 2:3] = jnp.sum(dconv * prev_two, axis=0, keepdims=True)
    dtaps_ref[0, 3:8] = jnp.zeros((5, width), F32)
    back_one = pltpu.roll(jnp.where(near_one, dconv, 0.0), rows - 1, 0)
    back_two = pltpu.roll(jnp.where(near_two, dconv, 0.0), rows - 2, 0)
    dv = (
        dv_ref[...]
        + taps_ref[0:1] * dconv
        + taps_ref[1:2] * back_one
        + taps_ref[2:3] * back_two
    )
    dqkv_ref[:, 0:qk_width] = dq.astype(BF16)
    dqkv_ref[:, qk_width : 2 * qk_width] = dk.astype(BF16)
    dqkv_ref[:, 2 * qk_width :] = dv.astype(BF16)


def seg_specs(rows):
    return [
        pl.BlockSpec((1, rows, 1), lambda m: (m, 0, 0)),
        pl.BlockSpec((1, 1, rows), lambda m: (m, 0, 0)),
    ]


def mix_forward(heads, micro, qkv, taps, segments):
    rows = qkv.shape[0] // micro
    width = heads * HEAD_SIZE
    return pl.pallas_call(
        partial(mix_kernel, heads),
        grid=(micro,),
        out_shape=jax.ShapeDtypeStruct((micro * rows, width), BF16),
        in_specs=[
            pl.BlockSpec((rows, qkv.shape[1]), lambda m: (m, 0)),
            pl.BlockSpec(taps.shape, lambda m: (0, 0)),
            *seg_specs(rows),
        ],
        out_specs=pl.BlockSpec((rows, width), lambda m: (m, 0)),
        scratch_shapes=[pltpu.VMEM((rows, width), F32)],
        compiler_params=pltpu.CompilerParams(vmem_limit_bytes=48 * 2**20),
    )(qkv, taps, segments[:, :, None], segments[:, None, :])


def mix_backward(heads, micro, qkv, dmixed, taps, segments):
    rows = qkv.shape[0] // micro
    width = heads * HEAD_SIZE
    return pl.pallas_call(
        partial(mix_back_kernel, heads),
        grid=(micro,),
        out_shape=(
            jax.ShapeDtypeStruct(qkv.shape, BF16),
            jax.ShapeDtypeStruct((micro, 8, width), F32),
        ),
        in_specs=[
            pl.BlockSpec((rows, qkv.shape[1]), lambda m: (m, 0)),
            pl.BlockSpec((rows, width), lambda m: (m, 0)),
            pl.BlockSpec(taps.shape, lambda m: (0, 0)),
            *seg_specs(rows),
        ],
        out_specs=(
            pl.BlockSpec((rows, qkv.shape[1]), lambda m: (m, 0)),
            pl.BlockSpec((1, 8, width), lambda m: (m, 0, 0)),
        ),
        scratch_shapes=[pltpu.VMEM((rows, width), F32)] * 3,
        compiler_params=pltpu.CompilerParams(vmem_limit_bytes=56 * 2**20),
    )(qkv, dmixed, taps, segments[:, :, None], segments[:, None, :])


def on_device(
    tokens,
    seq_order,
    seq_lengths,
    valid_count,
    teacher,
    norm_one,
    w_query,
    w_key,
    w_value,
    conv_taps,
    w_out,
    norm_two,
    w_gate,
    w_up,
    w_down,
):
    place = Place()
    seqs, y = place.seqs, place.y
    micro, rows_dev, model = tokens.shape[0], tokens.shape[2], tokens.shape[3]
    group = seqs * rows_dev
    rows = micro * group
    heads = HEADS // seqs
    qk_width = heads * FEAT
    width = heads * HEAD_SIZE
    slots = micro * place.fsdp * group

    def columns(weight):
        part = weight.shape[1] // seqs
        return lax.dynamic_slice_in_dim(weight, y * part, part, 1)

    shard_rows = w_query.shape[0]
    valid = valid_count[:, 0]
    coded = jnp.stack([valid // 16, valid % 16], axis=1).reshape(1, 2 * micro).astype(BF16)
    first_row = lax.broadcasted_iota(jnp.int32, (shard_rows, 2 * micro), 0) == 0
    small = jnp.concatenate(
        [
            norm_one[:, None],
            norm_two[:, None],
            conv_taps.T,
            jnp.where(first_row, coded, jnp.zeros_like(coded)),
        ],
        axis=1,
    )
    small = jnp.pad(small, ((0, 0), (0, SMALL - small.shape[1])))
    first_shard = jnp.concatenate(
        [columns(w_query), columns(w_key), columns(w_value), small], axis=1
    )
    first = lax.all_gather(first_shard, "fsdp", axis=0, tiled=True)
    out_part = spread_rows(place, w_out)
    down_part = spread_rows(place, w_down)
    out_w = plane_rows(place, lax.all_gather(out_part, "fsdp", axis=0, tiled=True))
    gate_w = lax.all_gather(columns(w_gate), "fsdp", axis=0, tiled=True)
    up_w = lax.all_gather(columns(w_up), "fsdp", axis=0, tiled=True)
    down_w = plane_rows(place, lax.all_gather(down_part, "fsdp", axis=0, tiled=True))

    qkv_width = 2 * qk_width + width
    qkv_w = first[:, :qkv_width]
    small_all = first[:, qkv_width : qkv_width + 16].astype(F32).T
    gain_one, gain_two = small_all[0], small_all[1]
    taps = lax.dynamic_slice_in_dim(small_all[2:5], y * width, width, 1)
    taps = jnp.pad(taps, ((0, 5), (0, 0)))
    coded_sum = jnp.sum(small_all[5 : 5 + 2 * micro], axis=1)
    total = 16.0 * jnp.sum(coded_sum[0::2]) + jnp.sum(coded_sum[1::2])
    scale = slots / total

    order = seq_order[:, 0, 0]
    order_all = jnp.stack(seq_pieces(place, order), axis=1)
    tokens_all = jnp.stack(seq_pieces(place, tokens[:, 0]), axis=1)
    local = jnp.arange(rows_dev, dtype=jnp.int32)
    pick_all = (order_all[..., None] == local).astype(BF16)
    packed = jnp.einsum("msij,msjd->msid", pick_all, tokens_all, preferred_element_type=BF16)
    packed = packed.reshape(rows, model)
    pick = (order[..., None] == local).astype(BF16)
    wanted = jnp.einsum("mij,mjd->mid", pick, teacher[:, 0], preferred_element_type=BF16)
    keep = (order + y * rows_dev < valid[:, None]).astype(F32)
    ends = jnp.cumsum(seq_lengths[:, 0], axis=1)
    positions = jnp.arange(group, dtype=jnp.int32)
    segments = jnp.sum((positions[None, :, None] >= ends[:, None, :]).astype(jnp.int32), axis=2)

    packed_f = packed.astype(F32)
    root_one = lax.rsqrt(jnp.mean(packed_f * packed_f, axis=1, keepdims=True) + EPSILON)
    n_one = (packed_f * root_one * gain_one).astype(BF16)
    qkv = dot(n_one, qkv_w).astype(BF16)
    mixed = mix_forward(heads, micro, qkv, taps, segments)

    def scatter(partial_rows):
        return seq_scatter(place, partial_rows.reshape(micro, seqs, rows_dev, model), 1)

    def gather(own_rows):
        return jnp.stack(seq_pieces(place, own_rows), axis=1).reshape(rows, model)

    packed_own = take(packed.reshape(micro, seqs, rows_dev, model), y, 1).astype(F32)
    resid = packed_own + scatter(dot(mixed, out_w))
    root_two = lax.rsqrt(jnp.mean(resid * resid, axis=2, keepdims=True) + EPSILON)
    n_two = gather((resid * root_two * gain_two).astype(BF16))
    gate = dot(n_two, gate_w)
    up = dot(n_two, up_w)
    sig = jax.nn.sigmoid(gate)
    hidden = (gate * sig * up).astype(BF16)
    result = resid + scatter(dot(hidden, down_w))
    output = jnp.einsum("mij,mid->mjd", pick, result.astype(BF16), preferred_element_type=BF16)
    error = (result - wanted.astype(F32)) * keep[..., None]
    squares = jnp.sum(error * error)
    loss = sum_everywhere(place, squares) / (total * model)

    d_result = scale * error
    d_low = gather(d_result.astype(BF16))
    grad_down = dot(hidden, d_low, ((0,), (0,))).astype(BF16)
    grad_down = grad_scatter(place, plane_grad_view(place, grad_down))
    d_hidden = dot(d_low, down_w, ((1,), (1,)))
    d_gate = (d_hidden * up * sig * (1.0 + gate * (1.0 - sig))).astype(BF16)
    d_up = (d_hidden * gate * sig).astype(BF16)

    def column_scatter(grad):
        view = grad.astype(BF16).reshape(Z_CHIPS, place.xs, CORES, shard_rows, grad.shape[1])
        return grad_scatter(place, view)

    grad_gate = column_scatter(dot(n_two, d_gate, ((0,), (0,))))
    grad_up = column_scatter(dot(n_two, d_up, ((0,), (0,))))
    d_n_two = scatter(dot(d_gate, gate_w, ((1,), (1,))) + dot(d_up, up_w, ((1,), (1,))))
    grad_norm_two = jnp.sum(d_n_two * resid * root_two, axis=(0, 1))
    d_scaled = d_n_two * gain_two
    d_resid = (
        d_result
        + root_two * d_scaled
        - resid * root_two**3 * jnp.mean(d_scaled * resid, axis=2, keepdims=True)
    )
    dm_low = gather(d_resid.astype(BF16))
    grad_out = dot(mixed, dm_low, ((0,), (0,))).astype(BF16)
    grad_out = grad_scatter(place, plane_grad_view(place, grad_out))
    d_mixed = dot(dm_low, out_w, ((1,), (1,)))
    d_qkv, d_taps = mix_backward(heads, micro, qkv, d_mixed, taps, segments)
    d_taps = jnp.sum(d_taps, axis=0)[:3]
    d_n_one_part = dot(d_qkv, qkv_w, ((1,), (1,)))
    grad_norm_one = jnp.sum(d_n_one_part * packed_f * root_one, axis=0)
    d_taps_wide = lax.dynamic_update_slice_in_dim(
        jnp.zeros((3, model), F32), d_taps, y * width, 1
    )
    extra = jnp.concatenate(
        [grad_norm_one[None], grad_norm_two[None], d_taps_wide, jnp.zeros((11, model), F32)]
    ).T
    extra = jnp.pad(extra.astype(BF16), ((0, 0), (0, SMALL - extra.shape[1])))
    grad_first = jnp.concatenate(
        [dot(n_one, d_qkv, ((0,), (0,))).astype(BF16), extra], axis=1
    )
    grad_first = column_scatter(grad_first)
    d_n_one = scatter(d_n_one_part)
    root_own = take(root_one.reshape(micro, seqs, rows_dev, 1), y, 1)
    d_scaled = d_n_one * gain_one
    d_packed = (
        d_resid
        + root_own * d_scaled
        - packed_own * root_own**3 * jnp.mean(d_scaled * packed_own, axis=2, keepdims=True)
    )
    input_grad = jnp.einsum(
        "mij,mid->mjd", pick, d_packed.astype(BF16), preferred_element_type=BF16
    )

    def join(parts):
        return jnp.concatenate(parts, axis=1).astype(F32)

    first_parts = seq_pieces(place, grad_first)
    extra_sum = sum(part[:, qkv_width:].astype(F32) for part in first_parts)
    return (
        output[:, None],
        input_grad[:, None],
        extra_sum[:, 0],
        join([part[:, :qk_width] for part in first_parts]),
        join([part[:, qk_width : 2 * qk_width] for part in first_parts]),
        join([part[:, 2 * qk_width : qkv_width] for part in first_parts]),
        extra_sum[:, 2:5].T,
        unspread_rows(place, grad_out),
        extra_sum[:, 1],
        join(seq_pieces(place, grad_gate)),
        join(seq_pieces(place, grad_up)),
        unspread_rows(place, grad_down),
        loss,
    )


def solution(mesh):
    rows = P(None, "fsdp", "seq", None)
    placed = (
        rows,
        rows,
        P(None, "fsdp", None),
        P(None, "fsdp"),
        rows,
        P("fsdp"),
        P("fsdp", None),
        P("fsdp", None),
        P("fsdp", None),
        P(None, "fsdp"),
        P("fsdp", None),
        P("fsdp"),
        P("fsdp", None),
        P("fsdp", None),
        P("fsdp", None),
    )
    return jax.shard_map(
        on_device,
        mesh=mesh,
        in_specs=placed,
        out_specs=(
            rows,
            rows,
            P("fsdp"),
            P("fsdp", None),
            P("fsdp", None),
            P("fsdp", None),
            P(None, "fsdp"),
            P("fsdp", None),
            P("fsdp"),
            P("fsdp", None),
            P("fsdp", None),
            P("fsdp", None),
            P(),
        ),
        check_vma=False,
    )
```

```python
from functools import partial

import jax
import jax.numpy as jnp
from jax import lax
from jax.experimental import pallas as pl
from jax.experimental.pallas import tpu as pltpu
from jax.sharding import PartitionSpec as P

HEADS = 16
FEAT = 16
HEAD_SIZE = 112
Z_CHIPS = 4
CORES = 2
SMALL = 128
GATHER_TILES = 528
EPSILON = 1e-05
BF16 = jnp.bfloat16
F32 = jnp.float32


def dot(left, right, dims=((1,), (0,))):
    return lax.dot_general(left, right, (dims, ((), ())), preferred_element_type=F32)


def take(array, index, axis):
    return lax.dynamic_index_in_dim(array, index, axis, keepdims=False)


def fence(*values):
    return lax.optimization_barrier(values)


class Place:
    def __init__(self):
        self.seqs = lax.axis_size("seq")
        self.fsdp = lax.axis_size("fsdp")
        self.xs = self.fsdp // (Z_CHIPS * CORES)
        self.y = lax.axis_index("seq")
        self.p = lax.axis_index("fsdp")
        self.c = self.p % CORES
        self.x = (self.p // CORES) % self.xs
        self.z = self.p // (CORES * self.xs)
        self.z_low_size = Z_CHIPS // self.seqs
        self.z_high = self.z // self.z_low_size
        self.turn = jnp.zeros((1, 128), F32)

    def in_turn(self, *values):
        *values, self.turn = fence(*values, self.turn)
        return values

    def index(self, z, x, c):
        return (z * self.xs + x) * CORES + c

    def everyone(self):
        for z in range(Z_CHIPS):
            for x in range(self.xs):
                for c in range(CORES):
                    yield z, x, c


def seq_send(place, value, k):
    pairs = [(i, (i + k) % place.seqs) for i in range(place.seqs)]
    return lax.ppermute(value, "seq", pairs)


def gather_seq(place, value):
    return [value] + [seq_send(place, value, k) for k in range(1, place.seqs)]


def in_order(place, pieces):
    if place.seqs == 2:
        first = place.y == 0
        return [
            jnp.where(first, pieces[0], pieces[1]),
            jnp.where(first, pieces[1], pieces[0]),
        ]
    stacked = jnp.stack(pieces)
    return [take(stacked, (place.y - j) % place.seqs, 0) for j in range(place.seqs)]


class Reduction:
    def __init__(self, place, grad, labels, order):
        self.place = place
        self.order = list(order)
        self.mine = {}
        self.parts = [(grad, tuple(labels))]

    def bit(self, label):
        return (self.place.p >> label) & 1

    def total(self, chosen):
        total = None
        for part, labels in self.parts:
            starts = [chosen[b] if b in chosen else 0 for b in labels] + [0, 0]
            sizes = [1 if b in chosen else 2 for b in labels] + list(part.shape[-2:])
            piece = lax.dynamic_slice(part, starts, sizes)
            left = [2 for b in labels if b not in chosen] + list(part.shape[-2:])
            piece = piece.reshape(left)
            total = piece if total is None else total.astype(F32) + piece.astype(F32)
        return total.astype(BF16)

    def left(self):
        return tuple(b for b in self.parts[0][1] if b not in self.mine)

    def pick(self, label):
        return self.total({**self.mine, label: 1 - self.bit(label)})

    def send(self, label, sent):
        pairs = [(i, i ^ (1 << label)) for i in range(self.place.fsdp)]
        got = lax.ppermute(sent, "fsdp", pairs)
        self.mine[label] = self.bit(label)
        self.parts.append((got, self.left()))

    def after(self, *values):
        got, labels = self.parts[-1]
        got, *values = self.place.in_turn(got, *values)
        self.parts[-1] = (got, labels)
        return values

    def start(self, *values):
        *done, label = self.order.pop(0)
        for bit in done:
            self.send(bit, self.pick(bit))
        sent, *values = self.place.in_turn(self.pick(label), *values)
        self.send(label, sent)
        return values

    def result(self):
        return self.total(self.mine)


def plane_pairs(place, k):
    pairs = []
    for y in range(place.seqs):
        for z, x, c in place.everyone():
            high, low = divmod(z, place.z_low_size)
            if high == y:
                other = ((y + k) % place.seqs) * place.z_low_size + low
                pairs.append(
                    (
                        y * place.fsdp + place.index(z, x, c),
                        y * place.fsdp + place.index(other, x, c),
                    )
                )
    return pairs


def spread_rows(place, shard):
    rows = shard.shape[0] // place.seqs
    pieces = shard.reshape(place.seqs, rows, shard.shape[1])
    part = take(pieces, place.y, 0)
    owner = place.z_high == place.y
    for k in range(1, place.seqs):
        sent = take(pieces, (place.y + k) % place.seqs, 0)
        got = lax.ppermute(sent, ("seq", "fsdp"), plane_pairs(place, k))
        part = jnp.where((place.z_high - place.y) % place.seqs == k, got, part)
    return part


def plane_rows(place, gathered):
    rows, columns = gathered.shape
    blocks = gathered.reshape(place.seqs, place.fsdp // place.seqs, -1, columns)
    return jnp.swapaxes(blocks, 0, 1).reshape(rows, columns)


def unspread_start(place, part):
    return gather_seq(place, part)


def unspread_end(place, planes):
    seqs = place.seqs
    part = planes[0]
    by_plane = jnp.stack(planes)
    shard = jnp.zeros((seqs,) + part.shape, part.dtype)
    mine = take(by_plane, (place.y - place.z_high) % seqs, 0)
    shard = lax.dynamic_update_index_in_dim(shard, mine, place.z_high, 0)
    for k in range(1, seqs):
        pairs = []
        for z, x, c in place.everyone():
            high, low = divmod(z, place.z_low_size)
            other = ((high + k) % seqs) * place.z_low_size + low
            pairs.append((place.index(z, x, c), place.index(other, x, c)))
        sent = take(by_plane, (place.y - place.z_high - k) % seqs, 0)
        got = lax.ppermute(sent, "fsdp", pairs)
        shard = lax.dynamic_update_index_in_dim(shard, got, (place.z_high - k) % seqs, 0)
    return shard.reshape(-1, part.shape[1]).astype(F32)


def sum_everywhere(place, value):
    for axis, count in (("fsdp", place.fsdp), ("seq", place.seqs)):
        bit = 1
        while bit < count:
            value = value + lax.ppermute(value, axis, [(i, i ^ bit) for i in range(count)])
            bit *= 2
    return value


def head_window(head):
    low = head * HEAD_SIZE // 128 * 128
    high = -(-(head + 1) * HEAD_SIZE // 128) * 128
    return low, high


def sigmoid(value):
    return 1.0 / (1.0 + jnp.exp(-value))


def conv_parts(values, taps_ref, seg_col):
    rows = values.shape[0]
    index = lax.broadcasted_iota(jnp.int32, (rows, 1), 0)
    near_one = (index >= 1) & (pltpu.roll(seg_col, 1, 0) == seg_col)
    near_two = (index >= 2) & (pltpu.roll(seg_col, 2, 0) == seg_col)
    prev_one = jnp.where(near_one, pltpu.roll(values, 1, 0), 0.0)
    prev_two = jnp.where(near_two, pltpu.roll(values, 2, 0), 0.0)
    conv = taps_ref[0:1] * values + taps_ref[1:2] * prev_one + taps_ref[2:3] * prev_two
    return conv, prev_one, prev_two, near_one, near_two


def masks(rows, seg_col, seg_row):
    at = lax.broadcasted_iota(jnp.int32, (rows, rows), 0)
    of = lax.broadcasted_iota(jnp.int32, (rows, rows), 1)
    return (seg_col == seg_row) & (at >= of)


def lanes_between(low, high, start, stop):
    lane = low + lax.broadcasted_iota(jnp.int32, (1, high - low), 1)
    return (lane >= start) & (lane < stop)


def relative(y_ref, seqs, piece):
    return lax.rem(y_ref[0] - piece + seqs, seqs)


def read_pieces(y_ref, ref):
    seqs = ref.shape[0]
    return jnp.concatenate([ref[relative(y_ref, seqs, s), 0] for s in range(seqs)], axis=0)


def write_pieces(y_ref, ref, value, low, high):
    seqs, rows = ref.shape[0], ref.shape[2]
    for s in range(seqs):
        ref[relative(y_ref, seqs, s), 0, :, low:high] = value[s * rows : (s + 1) * rows]


def mix_kernel(heads, y_ref, qkv_in, taps_ref, segc_ref, segr_ref, mixed_ref, qkv_ref, att_ref):
    qkv_ref[...] = read_pieces(y_ref, qkv_in)
    rows = qkv_ref.shape[0]
    qk_width = heads * FEAT
    width = heads * HEAD_SIZE
    seg_col = segc_ref[0]
    allowed = masks(rows, seg_col, segr_ref[0])
    queries = qkv_ref[:, 0:qk_width]
    keys = qkv_ref[:, qk_width : 2 * qk_width]
    for head in range(heads):
        mine = lanes_between(0, qk_width, head * FEAT, (head + 1) * FEAT)
        query = jnp.where(mine, queries, jnp.zeros_like(queries))
        scores = dot(query, keys, ((1,), (1,))) * 0.25
        kern = jnp.where(allowed, 1.0 + scores + 0.5 * scores * scores, 0.0)
        den = jnp.sum(kern, axis=1, keepdims=True)
        low, high = head_window(head)
        high = min(high, width)
        num = dot(kern.astype(BF16), qkv_ref[:, 2 * qk_width + low : 2 * qk_width + high])
        here = lanes_between(low, high, head * HEAD_SIZE, (head + 1) * HEAD_SIZE)
        att_ref[:, low:high] = jnp.where(here, num * (1.0 / den), att_ref[:, low:high])
    values = qkv_ref[:, 2 * qk_width : 2 * qk_width + width].astype(F32)
    conv = conv_parts(values, taps_ref, seg_col)[0]
    mixed = (att_ref[...] * conv * sigmoid(conv)).astype(BF16)
    write_pieces(y_ref, mixed_ref, mixed, 0, width)


def mix_back_kernel(
    heads, y_ref, qkv_in, dmixed_in, taps_ref, segc_ref, segr_ref, dqkv_ref, dtaps_ref,
    qkv_ref, dmixed_ref, att_ref, silu_ref, dv_ref,
):
    qkv_ref[...] = read_pieces(y_ref, qkv_in)
    dmixed_ref[...] = read_pieces(y_ref, dmixed_in).astype(F32)
    rows = qkv_ref.shape[0]
    qk_width = heads * FEAT
    width = heads * HEAD_SIZE
    seg_col = segc_ref[0]
    allowed = masks(rows, seg_col, segr_ref[0])
    queries = qkv_ref[:, 0:qk_width]
    keys = qkv_ref[:, qk_width : 2 * qk_width]
    values = qkv_ref[:, 2 * qk_width : 2 * qk_width + width].astype(F32)
    conv, prev_one, prev_two, near_one, near_two = conv_parts(values, taps_ref, seg_col)
    sig = sigmoid(conv)
    silu_ref[...] = dmixed_ref[...] * conv * sig
    dv_ref[...] = jnp.zeros_like(dv_ref)
    dq = jnp.zeros((rows, qk_width), F32)
    dk = jnp.zeros((rows, qk_width), F32)
    for head in range(heads):
        mine = lanes_between(0, qk_width, head * FEAT, (head + 1) * FEAT)
        query = jnp.where(mine, queries, jnp.zeros_like(queries))
        scores = dot(query, keys, ((1,), (1,))) * 0.25
        kern = jnp.where(allowed, 1.0 + scores + 0.5 * scores * scores, 0.0)
        inv_den = 1.0 / jnp.sum(kern, axis=1, keepdims=True)
        kern_low = kern.astype(BF16)
        low, high = head_window(head)
        high = min(high, width)
        value = qkv_ref[:, 2 * qk_width + low : 2 * qk_width + high]
        att = dot(kern_low, value) * inv_den
        here = lanes_between(low, high, head * HEAD_SIZE, (head + 1) * HEAD_SIZE)
        att_ref[:, low:high] = jnp.where(here, att, att_ref[:, low:high])
        datt = jnp.where(here, silu_ref[:, low:high], 0.0) * inv_den
        row_dot = jnp.sum(datt * att, axis=1, keepdims=True)
        datt_low = datt.astype(BF16)
        dkern = dot(datt_low, value, ((1,), (1,))) - row_dot
        dscores = jnp.where(allowed, dkern * (0.25 + 0.25 * scores), 0.0).astype(BF16)
        dq = dq + jnp.where(mine, dot(dscores, keys), 0.0)
        dk = dk + dot(dscores, query, ((0,), (0,)))
        dv_ref[:, low:high] += dot(kern_low, datt_low, ((0,), (0,)))
    dconv = dmixed_ref[...] * att_ref[...] * sig * (1.0 + conv * (1.0 - sig))
    dtaps_ref[0, 0:1] = jnp.sum(dconv * values, axis=0, keepdims=True)
    dtaps_ref[0, 1:2] = jnp.sum(dconv * prev_one, axis=0, keepdims=True)
    dtaps_ref[0, 2:3] = jnp.sum(dconv * prev_two, axis=0, keepdims=True)
    dtaps_ref[0, 3:8] = jnp.zeros((5, width), F32)
    back_one = pltpu.roll(jnp.where(near_one, dconv, 0.0), rows - 1, 0)
    back_two = pltpu.roll(jnp.where(near_two, dconv, 0.0), rows - 2, 0)
    dv = (
        dv_ref[...]
        + taps_ref[0:1] * dconv
        + taps_ref[1:2] * back_one
        + taps_ref[2:3] * back_two
    )
    write_pieces(y_ref, dqkv_ref, dq.astype(BF16), 0, qk_width)
    write_pieces(y_ref, dqkv_ref, dk.astype(BF16), qk_width, 2 * qk_width)
    write_pieces(y_ref, dqkv_ref, dv.astype(BF16), 2 * qk_width, 2 * qk_width + width)
    write_pieces(y_ref, dqkv_ref, jnp.zeros((rows, SMALL), BF16), 2 * qk_width + width, None)


def seg_specs(rows):
    return [
        pl.BlockSpec((1, rows, 1), lambda m: (m, 0, 0)),
        pl.BlockSpec((1, 1, rows), lambda m: (m, 0, 0)),
    ]


def piece_spec(shape):
    seqs, _, rows, width = shape
    return pl.BlockSpec((seqs, 1, rows, width), lambda m: (0, m, 0, 0))


def mix_forward(heads, y, qkv, taps, segments):
    seqs, micro, rows, qkv_width = qkv.shape
    group = seqs * rows
    width = heads * HEAD_SIZE
    return pl.pallas_call(
        partial(mix_kernel, heads),
        grid=(micro,),
        out_shape=jax.ShapeDtypeStruct((seqs, micro, rows, width), BF16),
        in_specs=[
            pl.BlockSpec(memory_space=pltpu.SMEM),
            piece_spec(qkv.shape),
            pl.BlockSpec(taps.shape, lambda m: (0, 0)),
            *seg_specs(group),
        ],
        out_specs=piece_spec((seqs, micro, rows, width)),
        scratch_shapes=[pltpu.VMEM((group, qkv_width), BF16), pltpu.VMEM((group, width), F32)],
        compiler_params=pltpu.CompilerParams(vmem_limit_bytes=48 * 2**20),
    )(y.reshape(1), qkv, taps, segments[:, :, None], segments[:, None, :])


def mix_backward(heads, y, qkv, dmixed, taps, segments):
    seqs, micro, rows, qkv_width = qkv.shape
    group = seqs * rows
    width = heads * HEAD_SIZE
    return pl.pallas_call(
        partial(mix_back_kernel, heads),
        grid=(micro,),
        out_shape=(
            jax.ShapeDtypeStruct(qkv.shape, BF16),
            jax.ShapeDtypeStruct((micro, 8, width), F32),
        ),
        in_specs=[
            pl.BlockSpec(memory_space=pltpu.SMEM),
            piece_spec(qkv.shape),
            piece_spec(dmixed.shape),
            pl.BlockSpec(taps.shape, lambda m: (0, 0)),
            *seg_specs(group),
        ],
        out_specs=(
            piece_spec(qkv.shape),
            pl.BlockSpec((1, 8, width), lambda m: (m, 0, 0)),
        ),
        scratch_shapes=[pltpu.VMEM((group, qkv_width), BF16)]
        + [pltpu.VMEM((group, width), F32)] * 4,
        compiler_params=pltpu.CompilerParams(vmem_limit_bytes=56 * 2**20),
    )(y.reshape(1), qkv, dmixed, taps, segments[:, :, None], segments[:, None, :])


class Gather:
    def __init__(self, arrays):
        self.shapes = [a.shape for a in arrays]
        self.joined = not any(a.shape[0] % 8 or a.shape[1] % 128 for a in arrays)
        if not self.joined:
            self.raw = [lax.all_gather(a, "fsdp", axis=0, tiled=True) for a in arrays]
            return
        counts = [a.size // 1024 for a in arrays]
        buffer = jnp.zeros((max(GATHER_TILES, sum(counts)), 8, 128), arrays[0].dtype)
        at = 0
        for a, count in zip(arrays, counts):
            t = a.reshape(a.shape[0] // 8, 8, a.shape[1] // 128, 128)
            t = jnp.swapaxes(t, 1, 2).reshape(-1, 8, 128)
            buffer = lax.dynamic_update_slice(buffer, t, (at, 0, 0))
            at += count
        self.raw = [lax.all_gather(buffer, "fsdp", axis=0, tiled=False)]

    def after(self, *values):
        count = len(self.raw)
        values = fence(*self.raw, *values)
        self.raw = list(values[:count])
        return values[count:]

    def arrays(self):
        if not self.joined:
            return self.raw
        gathered = []
        at = 0
        for rows, columns in self.shapes:
            count = rows * columns // 1024
            t = self.raw[0][:, at : at + count]
            t = t.reshape(-1, rows // 8, columns // 128, 8, 128)
            gathered.append(jnp.swapaxes(t, 2, 3).reshape(-1, columns))
            at += count
        return gathered


def on_device(
    tokens,
    seq_order,
    seq_lengths,
    valid_count,
    teacher,
    norm_one,
    w_query,
    w_key,
    w_value,
    conv_taps,
    w_out,
    norm_two,
    w_gate,
    w_up,
    w_down,
):
    place = Place()
    seqs, y = place.seqs, place.y
    micro, rows_dev, model = tokens.shape[0], tokens.shape[2], tokens.shape[3]
    group = seqs * rows_dev
    own_rows = micro * rows_dev
    heads = HEADS // seqs
    qk_width = heads * FEAT
    width = heads * HEAD_SIZE
    slots = micro * place.fsdp * group
    bits = place.fsdp.bit_length() - 1
    seq_bits = seqs.bit_length() - 1

    def columns(weight):
        part = weight.shape[1] // seqs
        return lax.dynamic_slice_in_dim(weight, y * part, part, 1)

    shard_rows = w_query.shape[0]
    valid = valid_count[:, 0]
    coded = jnp.stack([valid // 16, valid % 16], axis=1).reshape(1, 2 * micro).astype(BF16)
    first_row = lax.broadcasted_iota(jnp.int32, (shard_rows, 2 * micro), 0) == 0
    small = jnp.concatenate(
        [
            norm_one[:, None],
            norm_two[:, None],
            conv_taps.T,
            jnp.where(first_row, coded, jnp.zeros_like(coded)),
        ],
        axis=1,
    )
    small = jnp.pad(small, ((0, 0), (0, SMALL - small.shape[1])))
    first_shard = jnp.concatenate(
        [columns(w_query), columns(w_key), columns(w_value), small], axis=1
    )
    out_part = spread_rows(place, w_out)
    first, gate_w, out_w = Gather([first_shard, columns(w_gate), out_part]).arrays()
    down_part = spread_rows(place, w_down)
    late = Gather([columns(w_up), down_part])
    out_w = plane_rows(place, out_w)

    qkv_width = 2 * qk_width + width
    wide = qkv_width + SMALL
    small_all = first[:, qkv_width : qkv_width + 16].astype(F32).T
    gain_one, gain_two = small_all[0], small_all[1]
    taps = lax.dynamic_slice_in_dim(small_all[2:5], y * width, width, 1)
    taps = jnp.pad(taps, ((0, 5), (0, 0)))
    coded_sum = jnp.sum(small_all[5 : 5 + 2 * micro], axis=1)
    total = 16.0 * jnp.sum(coded_sum[0::2]) + jnp.sum(coded_sum[1::2])
    scale = slots / total

    order = seq_order[:, 0, 0]
    local = jnp.arange(rows_dev, dtype=jnp.int32)
    order_k = gather_seq(place, order)
    tokens_k = gather_seq(place, tokens[:, 0])
    picks = [(o[..., None] == local).astype(BF16) for o in order_k]
    pick = picks[0]
    packed_k = [
        jnp.einsum("mij,mjd->mid", o, t, preferred_element_type=BF16).reshape(own_rows, model)
        for o, t in zip(picks, tokens_k)
    ]
    wanted = jnp.einsum("mij,mjd->mid", pick, teacher[:, 0], preferred_element_type=BF16)
    wanted = wanted.reshape(own_rows, model)
    keep = (order + y * rows_dev < valid[:, None]).astype(F32).reshape(own_rows, 1)
    ends = jnp.cumsum(seq_lengths[:, 0], axis=1)
    positions = jnp.arange(group, dtype=jnp.int32)
    segments = jnp.sum((positions[None, :, None] >= ends[:, None, :]).astype(jnp.int32), axis=2)

    packed = jnp.concatenate(packed_k, axis=0)
    packed_f = packed.astype(F32)
    root_one = lax.rsqrt(jnp.mean(packed_f * packed_f, axis=1, keepdims=True) + EPSILON)
    n_one = (packed_f * root_one * gain_one).astype(BF16)
    qkv = dot(n_one, first).astype(BF16).reshape(seqs, micro, rows_dev, wide)
    mixed = mix_forward(heads, y, qkv, taps, segments).reshape(seqs * own_rows, width)

    def pieces(value):
        return [value[k * own_rows : (k + 1) * own_rows] for k in range(seqs)]

    def scatter(parts):
        got = [seq_send(place, parts[k].astype(BF16), seqs - k) for k in range(1, seqs)]
        return parts[0], got

    def project(rows_k, weight, dims=((1,), (0,))):
        parts = [None] * seqs
        for k in list(range(1, seqs)) + [0]:
            parts[k] = dot(rows_k[k], weight, dims)
        return parts

    packed_own = packed_k[0].astype(F32)
    own, got = scatter(project(pieces(mixed), out_w))
    resid = packed_own + own
    for part in got:
        resid = resid + part.astype(F32)
    root_two = lax.rsqrt(jnp.mean(resid * resid, axis=1, keepdims=True) + EPSILON)
    n_two_k = gather_seq(place, (resid * root_two * gain_two).astype(BF16))
    gate_k = [dot(n, gate_w) for n in n_two_k]
    gate_k = list(late.after(*gate_k))
    up_w, down_w = late.arrays()
    down_w = plane_rows(place, down_w)
    up_k = [dot(n, up_w) for n in n_two_k]
    sig_k = [jax.nn.sigmoid(g) for g in gate_k]
    hidden_k = [(g * s * u).astype(BF16) for g, s, u in zip(gate_k, sig_k, up_k)]
    own, got = scatter(project(hidden_k, down_w))
    result = resid + own
    for part in got:
        result = result + part.astype(F32)
    error = (result - wanted.astype(F32)) * keep
    d_result = scale * error
    d_low = d_result.astype(BF16)
    d_low_k = gather_seq(place, d_low)
    squares = sum_everywhere(place, jnp.sum(error * error, axis=(0, 1), keepdims=True))

    def to_given(value):
        value = value.astype(BF16).reshape(micro, rows_dev, model)
        return jnp.einsum("mij,mid->mjd", pick, value, preferred_element_type=BF16)

    output = to_given(result)

    def ffn_back(k, d_low):
        d_hidden = dot(d_low, down_w, ((1,), (1,)))
        gate, up, sig = gate_k[k], up_k[k], sig_k[k]
        d_gate = (d_hidden * up * sig * (1.0 + gate * (1.0 - sig))).astype(BF16)
        d_up = (d_hidden * gate * sig).astype(BF16)
        return d_gate, d_up

    column_labels = list(range(bits - 1, -1, -1))
    row_labels = list(range(bits - 1 - seq_bits, -1, -1)) + list(
        range(bits - 1, bits - 1 - seq_bits, -1)
    )
    x_bits = list(range(1, bits - 2))
    x_first = [[0], x_bits, [bits - 2], [bits - 1]]

    def by_rows(grad, order):
        view = grad.reshape([2] * bits + [grad.shape[0] // place.fsdp, grad.shape[1]])
        return Reduction(place, view, row_labels, order)

    def by_columns(grad, order):
        view = grad.reshape([2] * bits + [grad.shape[0] // place.fsdp, grad.shape[1]])
        return Reduction(place, view, column_labels, order)

    def weight_grad(left, right):
        return dot(left, right, ((0,), (0,))).astype(BF16)

    d_gate_own, d_up_own = ffn_back(0, d_low)
    hidden = jnp.concatenate(hidden_k, axis=0)
    n_two = jnp.concatenate(n_two_k, axis=0)
    d_gate_own, d_up_own, squares, *d_low_others = fence(
        d_gate_own, d_up_own, squares, *d_low_k[1:]
    )
    down = by_rows(weight_grad(hidden, jnp.concatenate([d_low, *d_low_others])), x_first)
    d_low_others = down.start(*d_low_others)
    d_pairs = [(d_gate_own, d_up_own)] + [
        ffn_back(k + 1, d) for k, d in enumerate(d_low_others)
    ]
    d_gate_k = [a for a, b in d_pairs]
    d_up_k = [b for a, b in d_pairs]
    d_gate = jnp.concatenate(d_gate_k, axis=0)
    d_up = jnp.concatenate(d_up_k, axis=0)
    gate_grad = weight_grad(n_two, d_gate)
    gate_grad, d_up, *d_both = fence(gate_grad, d_up, *d_gate_k, *d_up_k)
    gate_sum = lax.psum_scatter(gate_grad, "fsdp", scatter_dimension=0, tiled=True)
    d_both = down.after(*d_both)
    d_both = down.start(*d_both)
    d_gate_k, d_up_k = d_both[:seqs], d_both[seqs:]

    def ffn_part(k):
        return dot(d_gate_k[k], gate_w, ((1,), (1,))) + dot(d_up_k[k], up_w, ((1,), (1,)))

    parts = [ffn_part(k).astype(BF16) for k in range(1, seqs)]
    d_both = place.in_turn(*parts, d_up, *d_gate_k, *d_up_k)
    parts, d_up = d_both[: seqs - 1], d_both[seqs - 1]
    d_gate_k, d_up_k = d_both[seqs:-seqs], d_both[-seqs:]
    got = [seq_send(place, part, seqs - 1 - k) for k, part in enumerate(parts)]
    up = by_columns(weight_grad(n_two, d_up), x_first)
    d_gate_k[0], d_up_k[0] = up.start(d_gate_k[0], d_up_k[0])
    own = ffn_part(0)
    own, = up.after(own)
    own, *got = place.in_turn(own, *got)
    d_n_two = own
    for part in got:
        d_n_two = d_n_two + part.astype(F32)
    grad_norm_two = jnp.sum(d_n_two * resid * root_two, axis=0)
    d_scaled = d_n_two * gain_two
    d_resid = (
        d_result
        + root_two * d_scaled
        - resid * root_two**3 * jnp.mean(d_scaled * resid, axis=1, keepdims=True)
    )
    dm_own, = place.in_turn(d_resid.astype(BF16))
    dm_k = gather_seq(place, dm_own)
    dm_own, = up.start(dm_own)
    d_mixed_own = dot(dm_own, out_w, ((1,), (1,)))
    d_mixed_own, *dm_others = place.in_turn(d_mixed_own, *dm_k[1:])
    out = by_rows(weight_grad(mixed, jnp.concatenate([dm_own, *dm_others])), x_first)
    dm_others = out.start(*dm_others)
    d_mixed = jnp.concatenate(
        [d_mixed_own] + [dot(d, out_w, ((1,), (1,))) for d in dm_others]
    ).reshape(seqs, micro, rows_dev, width)
    d_mixed, = down.after(d_mixed)
    d_mixed, = down.start(d_mixed)
    d_mixed, = out.after(d_mixed)
    d_mixed, = out.start(d_mixed)
    d_qkv, d_taps = mix_backward(heads, y, qkv, d_mixed, taps, segments)
    d_qkv = d_qkv.reshape(seqs * own_rows, wide)
    d_taps = jnp.sum(d_taps, axis=0)[:3]
    others = [dot(d, first, ((1,), (1,))) for d in pieces(d_qkv)[1:]]
    sent = [part.astype(BF16) for part in others]
    *sent, d_qkv = place.in_turn(*sent, d_qkv)
    got = [seq_send(place, part, seqs - 1 - k) for k, part in enumerate(sent)]
    own = dot(d_qkv[:own_rows], first, ((1,), (1,)))
    grad_norm_one = sum(
        jnp.sum(part * (p.astype(F32) * r), axis=0)
        for part, p, r in zip([own, *others], packed_k, pieces(root_one))
    )
    d_taps_wide = lax.dynamic_update_slice_in_dim(
        jnp.zeros((3, model), F32), d_taps, y * width, 1
    )
    extra = jnp.concatenate(
        [grad_norm_one[None], grad_norm_two[None], d_taps_wide, jnp.zeros((3, model), F32)]
    )
    extra = jnp.pad(extra.T, ((0, 0), (qkv_width, SMALL - extra.shape[0])))
    grad_first = (dot(n_one, d_qkv, ((0,), (0,))) + extra).astype(BF16)
    grad_first, own = fence(grad_first, own)
    first_sum = lax.psum_scatter(grad_first, "fsdp", scatter_dimension=0, tiled=True)
    own, = up.after(own)
    own, = up.start(own)
    own, *got = place.in_turn(own, *got)

    d_n_one = own
    for part in got:
        d_n_one = d_n_one + part.astype(F32)
    root_own = root_one[:own_rows]
    d_scaled = d_n_one * gain_one
    d_packed = (
        d_resid
        + root_own * d_scaled
        - packed_own * root_own**3 * jnp.mean(d_scaled * packed_own, axis=1, keepdims=True)
    )
    def join(parts):
        return jnp.concatenate(parts, axis=1).astype(F32)

    def all_pieces(value):
        return in_order(place, gather_seq(place, value))

    input_grad = to_given(d_packed)
    input_grad, = down.after(input_grad)
    input_grad, = down.start(input_grad)
    out.after()
    out.start()
    up.after()
    up.start()
    out.after()
    out.start()
    gate_sum, = place.in_turn(gate_sum)
    gate_k = gather_seq(place, gate_sum)
    down.after()
    down_k = unspread_start(place, down.result())
    up.after()
    up_k = gather_seq(place, up.result())
    out.after()
    out_k = unspread_start(place, out.result())
    gate_k = place.in_turn(*gate_k)
    grad_gate = join(in_order(place, gate_k))
    down_k = place.in_turn(*down_k)
    grad_down = unspread_end(place, down_k)
    up_k = place.in_turn(*up_k)
    grad_up = join(in_order(place, up_k))
    out_k = place.in_turn(*out_k)
    grad_out = unspread_end(place, out_k)
    first_sum, = place.in_turn(first_sum)
    first_parts = all_pieces(first_sum)
    loss = (squares[0, 0] + place.turn[0, 0]) / (total * model)
    extra_sum = sum(part[:, qkv_width:].astype(F32) for part in first_parts)
    return (
        output[:, None],
        input_grad[:, None],
        extra_sum[:, 0],
        join([part[:, :qk_width] for part in first_parts]),
        join([part[:, qk_width : 2 * qk_width] for part in first_parts]),
        join([part[:, 2 * qk_width : qkv_width] for part in first_parts]),
        extra_sum[:, 2:5].T,
        grad_out,
        extra_sum[:, 1],
        grad_gate,
        grad_up,
        grad_down,
        loss,
    )


def solution(mesh):
    rows = P(None, "fsdp", "seq", None)
    placed = (
        rows,
        rows,
        P(None, "fsdp", None),
        P(None, "fsdp"),
        rows,
        P("fsdp"),
        P("fsdp", None),
        P("fsdp", None),
        P("fsdp", None),
        P(None, "fsdp"),
        P("fsdp", None),
        P("fsdp"),
        P("fsdp", None),
        P("fsdp", None),
        P("fsdp", None),
    )
    return jax.shard_map(
        on_device,
        mesh=mesh,
        in_specs=placed,
        out_specs=(
            rows,
            rows,
            P("fsdp"),
            P("fsdp", None),
            P("fsdp", None),
            P("fsdp", None),
            P(None, "fsdp"),
            P("fsdp", None),
            P("fsdp"),
            P("fsdp", None),
            P("fsdp", None),
            P("fsdp", None),
            P(),
        ),
        check_vma=False,
    )
```

```python
from functools import partial

import jax
import jax.numpy as jnp
from jax import lax
from jax.experimental import pallas as pl
from jax.experimental.pallas import tpu as pltpu
from jax.sharding import PartitionSpec as P

HEADS = 16
FEAT = 16
HEAD_SIZE = 112
Z_CHIPS = 4
CORES = 2
SMALL = 128
GATHER_TILES = 528
EPSILON = 1e-05
BF16 = jnp.bfloat16
F32 = jnp.float32


def dot(left, right, dims=((1,), (0,))):
    return lax.dot_general(left, right, (dims, ((), ())), preferred_element_type=F32)


def take(array, index, axis):
    return lax.dynamic_index_in_dim(array, index, axis, keepdims=False)


def fence(*values):
    return lax.optimization_barrier(values)


class Place:
    def __init__(self):
        self.seqs = lax.axis_size("seq")
        self.fsdp = lax.axis_size("fsdp")
        self.xs = self.fsdp // (Z_CHIPS * CORES)
        self.y = lax.axis_index("seq")
        self.p = lax.axis_index("fsdp")
        self.c = self.p % CORES
        self.x = (self.p // CORES) % self.xs
        self.z = self.p // (CORES * self.xs)
        self.z_low_size = Z_CHIPS // self.seqs
        self.z_high = self.z // self.z_low_size
        self.turn = jnp.zeros((1, 128), F32)

    def in_turn(self, *values):
        *values, self.turn = fence(*values, self.turn)
        return values

    def index(self, z, x, c):
        return (z * self.xs + x) * CORES + c

    def everyone(self):
        for z in range(Z_CHIPS):
            for x in range(self.xs):
                for c in range(CORES):
                    yield z, x, c


def seq_send(place, value, k):
    pairs = [(i, (i + k) % place.seqs) for i in range(place.seqs)]
    return lax.ppermute(value, "seq", pairs)


def gather_seq(place, value):
    return [value] + [seq_send(place, value, k) for k in range(1, place.seqs)]


def in_order(place, pieces):
    if place.seqs == 2:
        first = place.y == 0
        return [
            jnp.where(first, pieces[0], pieces[1]),
            jnp.where(first, pieces[1], pieces[0]),
        ]
    stacked = jnp.stack(pieces)
    return [take(stacked, (place.y - j) % place.seqs, 0) for j in range(place.seqs)]


class Reduction:
    def __init__(self, place, grad, labels, order):
        self.place = place
        self.order = list(order)
        self.mine = {}
        self.parts = [(grad, tuple(labels))]

    def bit(self, label):
        return (self.place.p >> label) & 1

    def total(self, chosen):
        total = None
        for part, labels in self.parts:
            starts = [chosen[b] if b in chosen else 0 for b in labels] + [0, 0]
            sizes = [1 if b in chosen else 2 for b in labels] + list(part.shape[-2:])
            piece = lax.dynamic_slice(part, starts, sizes)
            left = [2 for b in labels if b not in chosen] + list(part.shape[-2:])
            piece = piece.reshape(left)
            total = piece if total is None else total.astype(F32) + piece.astype(F32)
        return total.astype(BF16)

    def left(self):
        return tuple(b for b in self.parts[0][1] if b not in self.mine)

    def pick(self, label):
        return self.total({**self.mine, label: 1 - self.bit(label)})

    def send(self, label, sent):
        pairs = [(i, i ^ (1 << label)) for i in range(self.place.fsdp)]
        got = lax.ppermute(sent, "fsdp", pairs)
        self.mine[label] = self.bit(label)
        self.parts.append((got, self.left()))

    def after(self, *values):
        got, labels = self.parts[-1]
        got, *values = self.place.in_turn(got, *values)
        self.parts[-1] = (got, labels)
        return values

    def start(self, *values):
        *done, label = self.order.pop(0)
        for bit in done:
            self.send(bit, self.pick(bit))
        sent, *values = self.place.in_turn(self.pick(label), *values)
        self.send(label, sent)
        return values

    def result(self):
        return self.total(self.mine)


def plane_pairs(place, k):
    pairs = []
    for y in range(place.seqs):
        for z, x, c in place.everyone():
            high, low = divmod(z, place.z_low_size)
            if high == y:
                other = ((y + k) % place.seqs) * place.z_low_size + low
                pairs.append(
                    (
                        y * place.fsdp + place.index(z, x, c),
                        y * place.fsdp + place.index(other, x, c),
                    )
                )
    return pairs


def spread_rows(place, shard):
    rows = shard.shape[0] // place.seqs
    pieces = shard.reshape(place.seqs, rows, shard.shape[1])
    part = take(pieces, place.y, 0)
    owner = place.z_high == place.y
    for k in range(1, place.seqs):
        sent = take(pieces, (place.y + k) % place.seqs, 0)
        got = lax.ppermute(sent, ("seq", "fsdp"), plane_pairs(place, k))
        part = jnp.where((place.z_high - place.y) % place.seqs == k, got, part)
    return part


def plane_rows(place, gathered):
    rows, columns = gathered.shape
    blocks = gathered.reshape(place.seqs, place.fsdp // place.seqs, -1, columns)
    return jnp.swapaxes(blocks, 0, 1).reshape(rows, columns)


def unspread_start(place, part):
    return gather_seq(place, part)


def unspread_end(place, planes):
    seqs = place.seqs
    part = planes[0]
    by_plane = jnp.stack(planes)
    shard = jnp.zeros((seqs,) + part.shape, part.dtype)
    mine = take(by_plane, (place.y - place.z_high) % seqs, 0)
    shard = lax.dynamic_update_index_in_dim(shard, mine, place.z_high, 0)
    for k in range(1, seqs):
        pairs = []
        for z, x, c in place.everyone():
            high, low = divmod(z, place.z_low_size)
            other = ((high + k) % seqs) * place.z_low_size + low
            pairs.append((place.index(z, x, c), place.index(other, x, c)))
        sent = take(by_plane, (place.y - place.z_high - k) % seqs, 0)
        got = lax.ppermute(sent, "fsdp", pairs)
        shard = lax.dynamic_update_index_in_dim(shard, got, (place.z_high - k) % seqs, 0)
    return shard.reshape(-1, part.shape[1]).astype(F32)


def sum_over(axis, count, value):
    bit = 1
    while bit < count:
        value = value + lax.ppermute(value, axis, [(i, i ^ bit) for i in range(count)])
        bit *= 2
    return value


def head_window(head):
    low = head * HEAD_SIZE // 128 * 128
    high = -(-(head + 1) * HEAD_SIZE // 128) * 128
    return low, high


def sigmoid(value):
    return 1.0 / (1.0 + jnp.exp(-value))


def conv_parts(values, taps_ref, seg_col):
    rows = values.shape[0]
    index = lax.broadcasted_iota(jnp.int32, (rows, 1), 0)
    near_one = (index >= 1) & (pltpu.roll(seg_col, 1, 0) == seg_col)
    near_two = (index >= 2) & (pltpu.roll(seg_col, 2, 0) == seg_col)
    prev_one = jnp.where(near_one, pltpu.roll(values, 1, 0), 0.0)
    prev_two = jnp.where(near_two, pltpu.roll(values, 2, 0), 0.0)
    conv = taps_ref[0:1] * values + taps_ref[1:2] * prev_one + taps_ref[2:3] * prev_two
    return conv, prev_one, prev_two, near_one, near_two


def masks(rows, seg_col, seg_row):
    at = lax.broadcasted_iota(jnp.int32, (rows, rows), 0)
    of = lax.broadcasted_iota(jnp.int32, (rows, rows), 1)
    return (seg_col == seg_row) & (at >= of)


def lanes_between(low, high, start, stop):
    lane = low + lax.broadcasted_iota(jnp.int32, (1, high - low), 1)
    return (lane >= start) & (lane < stop)


def relative(y_ref, seqs, piece):
    return lax.rem(y_ref[0] - piece + seqs, seqs)


def read_pieces(y_ref, ref):
    seqs = ref.shape[0]
    return jnp.concatenate([ref[relative(y_ref, seqs, s), 0] for s in range(seqs)], axis=0)


def write_pieces(y_ref, ref, value, low, high):
    seqs, rows = ref.shape[0], ref.shape[2]
    for s in range(seqs):
        ref[relative(y_ref, seqs, s), 0, :, low:high] = value[s * rows : (s + 1) * rows]


def mix_kernel(heads, y_ref, qkv_in, taps_ref, segc_ref, segr_ref, mixed_ref, qkv_ref, att_ref):
    qkv_ref[...] = read_pieces(y_ref, qkv_in)
    rows = qkv_ref.shape[0]
    qk_width = heads * FEAT
    width = heads * HEAD_SIZE
    seg_col = segc_ref[0]
    allowed = masks(rows, seg_col, segr_ref[0])
    queries = qkv_ref[:, 0:qk_width]
    keys = qkv_ref[:, qk_width : 2 * qk_width]
    for head in range(heads):
        mine = lanes_between(0, qk_width, head * FEAT, (head + 1) * FEAT)
        query = jnp.where(mine, queries, jnp.zeros_like(queries))
        scores = dot(query, keys, ((1,), (1,))) * 0.25
        kern = jnp.where(allowed, 1.0 + scores + 0.5 * scores * scores, 0.0)
        den = jnp.sum(kern, axis=1, keepdims=True)
        low, high = head_window(head)
        high = min(high, width)
        num = dot(kern.astype(BF16), qkv_ref[:, 2 * qk_width + low : 2 * qk_width + high])
        here = lanes_between(low, high, head * HEAD_SIZE, (head + 1) * HEAD_SIZE)
        att_ref[:, low:high] = jnp.where(here, num * (1.0 / den), att_ref[:, low:high])
    values = qkv_ref[:, 2 * qk_width : 2 * qk_width + width].astype(F32)
    conv = conv_parts(values, taps_ref, seg_col)[0]
    mixed = (att_ref[...] * conv * sigmoid(conv)).astype(BF16)
    write_pieces(y_ref, mixed_ref, mixed, 0, width)


def mix_back_kernel(
    heads, y_ref, qkv_in, dmixed_in, taps_ref, segc_ref, segr_ref, dqkv_ref, dtaps_ref,
    qkv_ref, dmixed_ref, att_ref, silu_ref, dv_ref,
):
    qkv_ref[...] = read_pieces(y_ref, qkv_in)
    dmixed_ref[...] = read_pieces(y_ref, dmixed_in).astype(F32)
    rows = qkv_ref.shape[0]
    qk_width = heads * FEAT
    width = heads * HEAD_SIZE
    seg_col = segc_ref[0]
    allowed = masks(rows, seg_col, segr_ref[0])
    queries = qkv_ref[:, 0:qk_width]
    keys = qkv_ref[:, qk_width : 2 * qk_width]
    values = qkv_ref[:, 2 * qk_width : 2 * qk_width + width].astype(F32)
    conv, prev_one, prev_two, near_one, near_two = conv_parts(values, taps_ref, seg_col)
    sig = sigmoid(conv)
    silu_ref[...] = dmixed_ref[...] * conv * sig
    dv_ref[...] = jnp.zeros_like(dv_ref)
    dq = jnp.zeros((rows, qk_width), F32)
    dk = jnp.zeros((rows, qk_width), F32)
    for head in range(heads):
        mine = lanes_between(0, qk_width, head * FEAT, (head + 1) * FEAT)
        query = jnp.where(mine, queries, jnp.zeros_like(queries))
        scores = dot(query, keys, ((1,), (1,))) * 0.25
        kern = jnp.where(allowed, 1.0 + scores + 0.5 * scores * scores, 0.0)
        inv_den = 1.0 / jnp.sum(kern, axis=1, keepdims=True)
        kern_low = kern.astype(BF16)
        low, high = head_window(head)
        high = min(high, width)
        value = qkv_ref[:, 2 * qk_width + low : 2 * qk_width + high]
        att = dot(kern_low, value) * inv_den
        here = lanes_between(low, high, head * HEAD_SIZE, (head + 1) * HEAD_SIZE)
        att_ref[:, low:high] = jnp.where(here, att, att_ref[:, low:high])
        datt = jnp.where(here, silu_ref[:, low:high], 0.0) * inv_den
        row_dot = jnp.sum(datt * att, axis=1, keepdims=True)
        datt_low = datt.astype(BF16)
        dkern = dot(datt_low, value, ((1,), (1,))) - row_dot
        dscores = jnp.where(allowed, dkern * (0.25 + 0.25 * scores), 0.0).astype(BF16)
        dq = dq + jnp.where(mine, dot(dscores, keys), 0.0)
        dk = dk + dot(dscores, query, ((0,), (0,)))
        dv_ref[:, low:high] += dot(kern_low, datt_low, ((0,), (0,)))
    dconv = dmixed_ref[...] * att_ref[...] * sig * (1.0 + conv * (1.0 - sig))
    dtaps_ref[0, 0:1] = jnp.sum(dconv * values, axis=0, keepdims=True)
    dtaps_ref[0, 1:2] = jnp.sum(dconv * prev_one, axis=0, keepdims=True)
    dtaps_ref[0, 2:3] = jnp.sum(dconv * prev_two, axis=0, keepdims=True)
    dtaps_ref[0, 3:8] = jnp.zeros((5, width), F32)
    back_one = pltpu.roll(jnp.where(near_one, dconv, 0.0), rows - 1, 0)
    back_two = pltpu.roll(jnp.where(near_two, dconv, 0.0), rows - 2, 0)
    dv = (
        dv_ref[...]
        + taps_ref[0:1] * dconv
        + taps_ref[1:2] * back_one
        + taps_ref[2:3] * back_two
    )
    write_pieces(y_ref, dqkv_ref, dq.astype(BF16), 0, qk_width)
    write_pieces(y_ref, dqkv_ref, dk.astype(BF16), qk_width, 2 * qk_width)
    write_pieces(y_ref, dqkv_ref, dv.astype(BF16), 2 * qk_width, 2 * qk_width + width)
    write_pieces(y_ref, dqkv_ref, jnp.zeros((rows, SMALL), BF16), 2 * qk_width + width, None)


def seg_specs(rows):
    return [
        pl.BlockSpec((1, rows, 1), lambda m: (m, 0, 0)),
        pl.BlockSpec((1, 1, rows), lambda m: (m, 0, 0)),
    ]


def piece_spec(shape):
    seqs, _, rows, width = shape
    return pl.BlockSpec((seqs, 1, rows, width), lambda m: (0, m, 0, 0))


def mix_forward(heads, y, qkv, taps, segments):
    seqs, micro, rows, qkv_width = qkv.shape
    group = seqs * rows
    width = heads * HEAD_SIZE
    return pl.pallas_call(
        partial(mix_kernel, heads),
        grid=(micro,),
        out_shape=jax.ShapeDtypeStruct((seqs, micro, rows, width), BF16),
        in_specs=[
            pl.BlockSpec(memory_space=pltpu.SMEM),
            piece_spec(qkv.shape),
            pl.BlockSpec(taps.shape, lambda m: (0, 0)),
            *seg_specs(group),
        ],
        out_specs=piece_spec((seqs, micro, rows, width)),
        scratch_shapes=[pltpu.VMEM((group, qkv_width), BF16), pltpu.VMEM((group, width), F32)],
        compiler_params=pltpu.CompilerParams(vmem_limit_bytes=48 * 2**20),
    )(y.reshape(1), qkv, taps, segments[:, :, None], segments[:, None, :])


def mix_backward(heads, y, qkv, dmixed, taps, segments):
    seqs, micro, rows, qkv_width = qkv.shape
    group = seqs * rows
    width = heads * HEAD_SIZE
    return pl.pallas_call(
        partial(mix_back_kernel, heads),
        grid=(micro,),
        out_shape=(
            jax.ShapeDtypeStruct(qkv.shape, BF16),
            jax.ShapeDtypeStruct((micro, 8, width), F32),
        ),
        in_specs=[
            pl.BlockSpec(memory_space=pltpu.SMEM),
            piece_spec(qkv.shape),
            piece_spec(dmixed.shape),
            pl.BlockSpec(taps.shape, lambda m: (0, 0)),
            *seg_specs(group),
        ],
        out_specs=(
            piece_spec(qkv.shape),
            pl.BlockSpec((1, 8, width), lambda m: (m, 0, 0)),
        ),
        scratch_shapes=[pltpu.VMEM((group, qkv_width), BF16)]
        + [pltpu.VMEM((group, width), F32)] * 4,
        compiler_params=pltpu.CompilerParams(vmem_limit_bytes=56 * 2**20),
    )(y.reshape(1), qkv, dmixed, taps, segments[:, :, None], segments[:, None, :])


def copy_kernel(source_ref, out_ref):
    out_ref[...] = source_ref[...]


def take_tiles(whole, part, parts, order):
    shards, tiles = whole.shape[0], whole.shape[1] // parts
    return pl.pallas_call(
        copy_kernel,
        grid=(shards,),
        out_shape=jax.ShapeDtypeStruct((shards, tiles, 8, 128), whole.dtype),
        in_specs=[pl.BlockSpec((1, tiles, 8, 128), lambda i: (order(i), part, 0, 0))],
        out_specs=pl.BlockSpec((1, tiles, 8, 128), lambda i: (i, 0, 0, 0)),
        compiler_params=pltpu.CompilerParams(vmem_limit_bytes=48 * 2**20),
    )(whole)


def up_kernel(rows_ref, tiles_ref, gate_ref, up_ref, hidden_ref):
    count = tiles_ref.shape[2]
    depth = rows_ref.shape[1]
    weight = jnp.concatenate(
        [tiles_ref[:, :, i].reshape(depth, 128) for i in range(count)], axis=1
    )
    up = dot(rows_ref[...], weight)
    gate = gate_ref[...]
    up_ref[...] = up
    hidden_ref[...] = (gate * sigmoid(gate) * up).astype(BF16)


def up_hidden(rows, whole, shape, gate, count=5):
    row_tiles, columns = shape[0] // 8, shape[1]
    tiles = whole.reshape(whole.shape[0], 2 * row_tiles, columns // 128, 8, 128)
    block = (whole.shape[0], row_tiles, count, 8, 128)
    wide = pl.BlockSpec((rows.shape[0], count * 128), lambda j: (0, j))
    return pl.pallas_call(
        up_kernel,
        grid=(-(-columns // (count * 128)),),
        out_shape=(
            jax.ShapeDtypeStruct((rows.shape[0], columns), F32),
            jax.ShapeDtypeStruct((rows.shape[0], columns), BF16),
        ),
        in_specs=[
            pl.BlockSpec(rows.shape, lambda j: (0, 0)),
            pl.BlockSpec(block, lambda j: (0, 0, j, 0, 0)),
            wide,
        ],
        out_specs=(wide, wide),
        compiler_params=pltpu.CompilerParams(vmem_limit_bytes=48 * 2**20),
    )(rows, tiles, gate)


class Gather:
    def __init__(self, arrays):
        self.shapes = [a.shape for a in arrays]
        self.joined = not any(a.shape[0] % 8 or a.shape[1] % 128 for a in arrays)
        if not self.joined:
            self.raw = [lax.all_gather(a, "fsdp", axis=0, tiled=True) for a in arrays]
            return
        counts = [a.size // 1024 for a in arrays]
        buffer = jnp.zeros((max(GATHER_TILES, sum(counts)), 8, 128), arrays[0].dtype)
        at = 0
        for a, count in zip(arrays, counts):
            t = a.reshape(a.shape[0] // 8, 8, a.shape[1] // 128, 128)
            t = jnp.swapaxes(t, 1, 2).reshape(-1, 8, 128)
            buffer = lax.dynamic_update_slice(buffer, t, (at, 0, 0))
            at += count
        self.raw = [lax.all_gather(buffer, "fsdp", axis=0, tiled=False)]

    def after(self, *values):
        count = len(self.raw)
        values = fence(*self.raw, *values)
        self.raw = list(values[:count])
        return values[count:]

    def arrays(self):
        if not self.joined:
            return self.raw
        gathered = []
        at = 0
        for rows, columns in self.shapes:
            count = rows * columns // 1024
            t = self.raw[0][:, at : at + count]
            t = t.reshape(-1, rows // 8, columns // 128, 8, 128)
            gathered.append(jnp.swapaxes(t, 2, 3).reshape(-1, columns))
            at += count
        return gathered


def on_device(
    tokens,
    seq_order,
    seq_lengths,
    valid_count,
    teacher,
    norm_one,
    w_query,
    w_key,
    w_value,
    conv_taps,
    w_out,
    norm_two,
    w_gate,
    w_up,
    w_down,
):
    place = Place()
    seqs, y = place.seqs, place.y
    micro, rows_dev, model = tokens.shape[0], tokens.shape[2], tokens.shape[3]
    group = seqs * rows_dev
    own_rows = micro * rows_dev
    heads = HEADS // seqs
    qk_width = heads * FEAT
    width = heads * HEAD_SIZE
    slots = micro * place.fsdp * group
    bits = place.fsdp.bit_length() - 1
    seq_bits = seqs.bit_length() - 1

    def columns(weight):
        part = weight.shape[1] // seqs
        return lax.dynamic_slice_in_dim(weight, y * part, part, 1)

    shard_rows = w_query.shape[0]
    valid = valid_count[:, 0]
    coded = jnp.stack([valid // 16, valid % 16], axis=1).reshape(1, 2 * micro).astype(BF16)
    first_row = lax.broadcasted_iota(jnp.int32, (shard_rows, 2 * micro), 0) == 0
    small = jnp.concatenate(
        [
            norm_one[:, None],
            norm_two[:, None],
            conv_taps.T,
            jnp.where(first_row, coded, jnp.zeros_like(coded)),
        ],
        axis=1,
    )
    small = jnp.pad(small, ((0, 0), (0, SMALL - small.shape[1])))
    first_shard = jnp.concatenate(
        [columns(w_query), columns(w_key), columns(w_value), small], axis=1
    )
    out_part = spread_rows(place, w_out)
    first, gate_w, out_w = Gather([first_shard, columns(w_gate), out_part]).arrays()
    down_part = spread_rows(place, w_down)
    late = Gather([columns(w_up), down_part])
    out_w = plane_rows(place, out_w)

    qkv_width = 2 * qk_width + width
    wide = qkv_width + SMALL
    small_all = first[:, qkv_width : qkv_width + 16].astype(F32).T
    gain_one, gain_two = small_all[0], small_all[1]
    taps = lax.dynamic_slice_in_dim(small_all[2:5], y * width, width, 1)
    taps = jnp.pad(taps, ((0, 5), (0, 0)))
    coded_sum = jnp.sum(small_all[5 : 5 + 2 * micro], axis=1)
    total = 16.0 * jnp.sum(coded_sum[0::2]) + jnp.sum(coded_sum[1::2])
    scale = slots / total

    order = seq_order[:, 0, 0]
    local = jnp.arange(rows_dev, dtype=jnp.int32)
    order_k = gather_seq(place, order)
    tokens_k = gather_seq(place, tokens[:, 0])
    picks = [(o[..., None] == local).astype(BF16) for o in order_k]
    pick = picks[0]
    packed_k = [
        jnp.einsum("mij,mjd->mid", o, t, preferred_element_type=BF16).reshape(own_rows, model)
        for o, t in zip(picks, tokens_k)
    ]
    wanted = jnp.einsum("mij,mjd->mid", pick, teacher[:, 0], preferred_element_type=BF16)
    wanted = wanted.reshape(own_rows, model)
    keep = (order + y * rows_dev < valid[:, None]).astype(F32).reshape(own_rows, 1)
    ends = jnp.cumsum(seq_lengths[:, 0], axis=1)
    positions = jnp.arange(group, dtype=jnp.int32)
    segments = jnp.sum((positions[None, :, None] >= ends[:, None, :]).astype(jnp.int32), axis=2)

    packed = jnp.concatenate(packed_k, axis=0)
    packed_f = packed.astype(F32)
    root_one = lax.rsqrt(jnp.mean(packed_f * packed_f, axis=1, keepdims=True) + EPSILON)
    n_one = (packed_f * root_one * gain_one).astype(BF16)
    qkv = dot(n_one, first).astype(BF16).reshape(seqs, micro, rows_dev, wide)
    mixed = mix_forward(heads, y, qkv, taps, segments).reshape(seqs * own_rows, width)

    def pieces(value):
        return [value[k * own_rows : (k + 1) * own_rows] for k in range(seqs)]

    def scatter(parts):
        got = [seq_send(place, parts[k].astype(BF16), seqs - k) for k in range(1, seqs)]
        return parts[0], got

    def project(rows_k, weight, dims=((1,), (0,))):
        parts = [None] * seqs
        for k in list(range(1, seqs)) + [0]:
            parts[k] = dot(rows_k[k], weight, dims)
        return parts

    packed_own = packed_k[0].astype(F32)
    own, got = scatter(project(pieces(mixed), out_w))
    own, *got = fence(own, *got)
    resid = packed_own + own
    for part in got:
        resid = resid + part.astype(F32)
    root_two = lax.rsqrt(jnp.mean(resid * resid, axis=1, keepdims=True) + EPSILON)
    n_two_k = gather_seq(place, (resid * root_two * gain_two).astype(BF16))
    gate_k = [dot(n, gate_w) for n in n_two_k]
    gate_k = list(late.after(*gate_k))
    whole = late.raw[0]
    direct = late.joined and whole.shape[1] == 2 * late.shapes[0][0] * late.shapes[0][1] // 1024
    up_k, hidden_k = [None] * seqs, [None] * seqs
    if direct:
        for k in list(range(1, seqs)) + [0]:
            up_k[k], hidden_k[k] = up_hidden(n_two_k[k], whole, late.shapes[0], gate_k[k])
        per = place.fsdp // seqs
        tiles = take_tiles(whole, 1, 2, lambda i: (i % seqs) * per + i // seqs)
        rows_down, columns_down = late.shapes[1]
        tiles = tiles.reshape(-1, rows_down // 8, columns_down // 128, 8, 128)
        down_w = jnp.swapaxes(tiles, 2, 3).reshape(-1, columns_down)
    else:
        up_w, down_w = late.arrays()
        down_w = plane_rows(place, down_w)
        for k in range(seqs):
            up_k[k] = dot(n_two_k[k], up_w)
            hidden_k[k] = (gate_k[k] * jax.nn.sigmoid(gate_k[k]) * up_k[k]).astype(BF16)
    sig_k = [jax.nn.sigmoid(g) for g in gate_k]
    own, got = scatter(project(hidden_k, down_w))
    if direct:
        late.raw[0], own = fence(late.raw[0], own)
        up_w, _ = late.arrays()
    own, up_w, *got = fence(own, up_w, *got)
    result = resid + own
    for part in got:
        result = result + part.astype(F32)
    error = (result - wanted.astype(F32)) * keep
    d_result = scale * error
    d_low = d_result.astype(BF16)
    d_low_k = gather_seq(place, d_low)
    squares = sum_over("fsdp", place.fsdp, jnp.sum(error * error, axis=(0, 1), keepdims=True))

    def to_given(value):
        value = value.astype(BF16).reshape(micro, rows_dev, model)
        return jnp.einsum("mij,mid->mjd", pick, value, preferred_element_type=BF16)

    output = to_given(result)

    def ffn_back(k, d_low):
        d_hidden = dot(d_low, down_w, ((1,), (1,)))
        gate, up, sig = gate_k[k], up_k[k], sig_k[k]
        d_gate = (d_hidden * up * sig * (1.0 + gate * (1.0 - sig))).astype(BF16)
        d_up = (d_hidden * gate * sig).astype(BF16)
        return d_gate, d_up

    column_labels = list(range(bits - 1, -1, -1))
    row_labels = list(range(bits - 1 - seq_bits, -1, -1)) + list(
        range(bits - 1, bits - 1 - seq_bits, -1)
    )
    x_bits = list(range(1, bits - 2))
    x_first = [[0], x_bits, [bits - 2], [bits - 1]]

    def by_rows(grad, order):
        view = grad.reshape([2] * bits + [grad.shape[0] // place.fsdp, grad.shape[1]])
        return Reduction(place, view, row_labels, order)

    def by_columns(grad, order):
        view = grad.reshape([2] * bits + [grad.shape[0] // place.fsdp, grad.shape[1]])
        return Reduction(place, view, column_labels, order)

    def weight_grad(left, right):
        return dot(left, right, ((0,), (0,))).astype(BF16)

    d_gate_own, d_up_own = ffn_back(0, d_low)
    hidden = jnp.concatenate(hidden_k, axis=0)
    n_two = jnp.concatenate(n_two_k, axis=0)
    d_gate_own, d_up_own, squares, *d_low_others = fence(
        d_gate_own, d_up_own, squares, *d_low_k[1:]
    )
    down = by_rows(weight_grad(hidden, jnp.concatenate([d_low, *d_low_others])), x_first)
    d_low_others = down.start(*d_low_others)
    d_pairs = [(d_gate_own, d_up_own)] + [
        ffn_back(k + 1, d) for k, d in enumerate(d_low_others)
    ]
    d_gate_k = [a for a, b in d_pairs]
    d_up_k = [b for a, b in d_pairs]
    d_gate = jnp.concatenate(d_gate_k, axis=0)
    d_up = jnp.concatenate(d_up_k, axis=0)
    gate_grad = weight_grad(n_two, d_gate)
    gate_grad, d_up, *d_both = fence(gate_grad, d_up, *d_gate_k, *d_up_k)
    gate_sum = lax.psum_scatter(gate_grad, "fsdp", scatter_dimension=0, tiled=True)
    d_both = down.after(*d_both)
    d_both = down.start(*d_both)
    d_gate_k, d_up_k = d_both[:seqs], d_both[seqs:]

    def ffn_part(k):
        return dot(d_gate_k[k], gate_w, ((1,), (1,))) + dot(d_up_k[k], up_w, ((1,), (1,)))

    parts = [ffn_part(k).astype(BF16) for k in range(1, seqs)]
    d_both = place.in_turn(*parts, d_up, *d_gate_k, *d_up_k)
    parts, d_up = d_both[: seqs - 1], d_both[seqs - 1]
    d_gate_k, d_up_k = d_both[seqs:-seqs], d_both[-seqs:]
    got = [seq_send(place, part, seqs - 1 - k) for k, part in enumerate(parts)]
    up = by_columns(weight_grad(n_two, d_up), x_first)
    d_gate_k[0], d_up_k[0] = up.start(d_gate_k[0], d_up_k[0])
    own = ffn_part(0)
    own, = up.after(own)
    own, *got = place.in_turn(own, *got)
    d_n_two = own
    for part in got:
        d_n_two = d_n_two + part.astype(F32)
    grad_norm_two = jnp.sum(d_n_two * resid * root_two, axis=0)
    d_scaled = d_n_two * gain_two
    d_resid = (
        d_result
        + root_two * d_scaled
        - resid * root_two**3 * jnp.mean(d_scaled * resid, axis=1, keepdims=True)
    )
    dm_own, = place.in_turn(d_resid.astype(BF16))
    dm_k = gather_seq(place, dm_own)
    dm_own, = up.start(dm_own)
    d_mixed_own = dot(dm_own, out_w, ((1,), (1,)))
    squares = sum_over("seq", seqs, squares)
    d_mixed_own, squares, *dm_others = place.in_turn(d_mixed_own, squares, *dm_k[1:])
    out = by_rows(weight_grad(mixed, jnp.concatenate([dm_own, *dm_others])), x_first)
    dm_others = out.start(*dm_others)
    d_mixed = jnp.concatenate(
        [d_mixed_own] + [dot(d, out_w, ((1,), (1,))) for d in dm_others]
    ).reshape(seqs, micro, rows_dev, width)
    d_mixed, = down.after(d_mixed)
    d_mixed, = down.start(d_mixed)
    d_mixed, = out.after(d_mixed)
    d_mixed, = out.start(d_mixed)
    d_qkv, d_taps = mix_backward(heads, y, qkv, d_mixed, taps, segments)
    d_qkv = d_qkv.reshape(seqs * own_rows, wide)
    d_taps = jnp.sum(d_taps, axis=0)[:3]
    others = [dot(d, first, ((1,), (1,))) for d in pieces(d_qkv)[1:]]
    sent = [part.astype(BF16) for part in others]
    *sent, d_qkv = place.in_turn(*sent, d_qkv)
    got = [seq_send(place, part, seqs - 1 - k) for k, part in enumerate(sent)]
    own = dot(d_qkv[:own_rows], first, ((1,), (1,)))
    grad_norm_one = sum(
        jnp.sum(part * (p.astype(F32) * r), axis=0)
        for part, p, r in zip([own, *others], packed_k, pieces(root_one))
    )
    d_taps_wide = lax.dynamic_update_slice_in_dim(
        jnp.zeros((3, model), F32), d_taps, y * width, 1
    )
    extra = jnp.concatenate(
        [grad_norm_one[None], grad_norm_two[None], d_taps_wide, jnp.zeros((3, model), F32)]
    )
    extra = jnp.pad(extra.T, ((0, 0), (qkv_width, SMALL - extra.shape[0])))
    grad_first = (dot(n_one, d_qkv, ((0,), (0,))) + extra).astype(BF16)
    grad_first, own = fence(grad_first, own)
    first_sum = lax.psum_scatter(grad_first, "fsdp", scatter_dimension=0, tiled=True)
    own, *got = place.in_turn(own, *got)

    d_n_one = own
    for part in got:
        d_n_one = d_n_one + part.astype(F32)
    root_own = root_one[:own_rows]
    d_scaled = d_n_one * gain_one
    d_packed = (
        d_resid
        + root_own * d_scaled
        - packed_own * root_own**3 * jnp.mean(d_scaled * packed_own, axis=1, keepdims=True)
    )
    def join(parts):
        return jnp.concatenate(parts, axis=1).astype(F32)

    d_packed, = up.after(d_packed)
    d_packed, = up.start(d_packed)
    d_packed, gate_sum = place.in_turn(d_packed, gate_sum)
    gate_k = gather_seq(place, gate_sum)
    input_grad = to_given(d_packed)
    down.after()
    down.start()
    out.after()
    out.start()
    up.after()
    up.start()
    down.after()
    down_k = unspread_start(place, down.result())
    gate_k = place.in_turn(*gate_k)
    grad_gate = join(in_order(place, gate_k))
    out.after()
    out.start()
    down_k = place.in_turn(*down_k)
    grad_down = unspread_end(place, down_k)
    up.after()
    up_k = gather_seq(place, up.result())
    out.after()
    out_k = unspread_start(place, out.result())
    first_sum, = place.in_turn(first_sum)
    first_k = gather_seq(place, first_sum)
    out_k = place.in_turn(*out_k)
    grad_out = unspread_end(place, out_k)
    up_k = place.in_turn(*up_k)
    grad_up = join(in_order(place, up_k))
    first_parts = in_order(place, first_k)
    loss = (squares[0, 0] + place.turn[0, 0]) / (total * model)
    extra_sum = sum(part[:, qkv_width:].astype(F32) for part in first_parts)
    return (
        output[:, None],
        input_grad[:, None],
        extra_sum[:, 0],
        join([part[:, :qk_width] for part in first_parts]),
        join([part[:, qk_width : 2 * qk_width] for part in first_parts]),
        join([part[:, 2 * qk_width : qkv_width] for part in first_parts]),
        extra_sum[:, 2:5].T,
        grad_out,
        extra_sum[:, 1],
        grad_gate,
        grad_up,
        grad_down,
        loss,
    )


def solution(mesh):
    rows = P(None, "fsdp", "seq", None)
    placed = (
        rows,
        rows,
        P(None, "fsdp", None),
        P(None, "fsdp"),
        rows,
        P("fsdp"),
        P("fsdp", None),
        P("fsdp", None),
        P("fsdp", None),
        P(None, "fsdp"),
        P("fsdp", None),
        P("fsdp"),
        P("fsdp", None),
        P("fsdp", None),
        P("fsdp", None),
    )
    return jax.shard_map(
        on_device,
        mesh=mesh,
        in_specs=placed,
        out_specs=(
            rows,
            rows,
            P("fsdp"),
            P("fsdp", None),
            P("fsdp", None),
            P("fsdp", None),
            P(None, "fsdp"),
            P("fsdp", None),
            P("fsdp"),
            P("fsdp", None),
            P("fsdp", None),
            P("fsdp", None),
            P(),
        ),
        check_vma=False,
    )
```

```python
from functools import partial

import jax
import jax.numpy as jnp
from jax import lax
from jax.experimental import pallas as pl
from jax.experimental.pallas import tpu as pltpu
from jax.sharding import PartitionSpec as P

HEADS = 16
FEAT = 16
HEAD_SIZE = 112
Z_CHIPS = 4
CORES = 2
SMALL = 128
GATHER_TILES = 528
EPSILON = 1e-05
BF16 = jnp.bfloat16
F32 = jnp.float32


def dot(left, right, dims=((1,), (0,))):
    return lax.dot_general(left, right, (dims, ((), ())), preferred_element_type=F32)


def take(array, index, axis):
    return lax.dynamic_index_in_dim(array, index, axis, keepdims=False)


def fence(*values):
    return lax.optimization_barrier(values)


class Place:
    def __init__(self):
        self.seqs = lax.axis_size("seq")
        self.fsdp = lax.axis_size("fsdp")
        self.xs = self.fsdp // (Z_CHIPS * CORES)
        self.y = lax.axis_index("seq")
        self.p = lax.axis_index("fsdp")
        self.c = self.p % CORES
        self.x = (self.p // CORES) % self.xs
        self.z = self.p // (CORES * self.xs)
        self.z_low_size = Z_CHIPS // self.seqs
        self.z_high = self.z // self.z_low_size
        self.turn = jnp.zeros((1, 128), F32)

    def in_turn(self, *values):
        *values, self.turn = fence(*values, self.turn)
        return values

    def index(self, z, x, c):
        return (z * self.xs + x) * CORES + c

    def everyone(self):
        for z in range(Z_CHIPS):
            for x in range(self.xs):
                for c in range(CORES):
                    yield z, x, c


def seq_send(place, value, k):
    pairs = [(i, (i + k) % place.seqs) for i in range(place.seqs)]
    return lax.ppermute(value, "seq", pairs)


def gather_seq(place, value):
    return [value] + [seq_send(place, value, k) for k in range(1, place.seqs)]


def in_order(place, pieces):
    if place.seqs == 2:
        first = place.y == 0
        return [
            jnp.where(first, pieces[0], pieces[1]),
            jnp.where(first, pieces[1], pieces[0]),
        ]
    stacked = jnp.stack(pieces)
    return [take(stacked, (place.y - j) % place.seqs, 0) for j in range(place.seqs)]


class Reduction:
    def __init__(self, place, grad, labels, order):
        self.place = place
        self.order = list(order)
        self.mine = {}
        self.parts = [(grad, tuple(labels))]

    def bit(self, label):
        return (self.place.p >> label) & 1

    def total(self, chosen):
        total = None
        for part, labels in self.parts:
            starts = [chosen[b] if b in chosen else 0 for b in labels] + [0, 0]
            sizes = [1 if b in chosen else 2 for b in labels] + list(part.shape[-2:])
            piece = lax.dynamic_slice(part, starts, sizes)
            left = [2 for b in labels if b not in chosen] + list(part.shape[-2:])
            piece = piece.reshape(left)
            total = piece if total is None else total.astype(F32) + piece.astype(F32)
        return total.astype(BF16)

    def left(self):
        return tuple(b for b in self.parts[0][1] if b not in self.mine)

    def pick(self, label):
        return self.total({**self.mine, label: 1 - self.bit(label)})

    def send(self, label, sent):
        pairs = [(i, i ^ (1 << label)) for i in range(self.place.fsdp)]
        got = lax.ppermute(sent, "fsdp", pairs)
        self.mine[label] = self.bit(label)
        self.parts.append((got, self.left()))

    def after(self, *values):
        got, labels = self.parts[-1]
        got, *values = self.place.in_turn(got, *values)
        self.parts[-1] = (got, labels)
        return values

    def start(self, *values):
        *done, label = self.order.pop(0)
        for bit in done:
            self.send(bit, self.pick(bit))
        sent, *values = self.place.in_turn(self.pick(label), *values)
        self.send(label, sent)
        return values

    def result(self):
        return self.total(self.mine)


def plane_pairs(place, k):
    pairs = []
    for y in range(place.seqs):
        for z, x, c in place.everyone():
            high, low = divmod(z, place.z_low_size)
            if high == y:
                other = ((y + k) % place.seqs) * place.z_low_size + low
                pairs.append(
                    (
                        y * place.fsdp + place.index(z, x, c),
                        y * place.fsdp + place.index(other, x, c),
                    )
                )
    return pairs


def spread_rows(place, shard):
    rows = shard.shape[0] // place.seqs
    pieces = shard.reshape(place.seqs, rows, shard.shape[1])
    part = take(pieces, place.y, 0)
    owner = place.z_high == place.y
    for k in range(1, place.seqs):
        sent = take(pieces, (place.y + k) % place.seqs, 0)
        got = lax.ppermute(sent, ("seq", "fsdp"), plane_pairs(place, k))
        part = jnp.where((place.z_high - place.y) % place.seqs == k, got, part)
    return part


def plane_rows(place, gathered):
    rows, columns = gathered.shape
    blocks = gathered.reshape(place.seqs, place.fsdp // place.seqs, -1, columns)
    return jnp.swapaxes(blocks, 0, 1).reshape(rows, columns)


def unspread_start(place, part):
    return gather_seq(place, part)


def unspread_end(place, planes):
    seqs = place.seqs
    part = planes[0]
    by_plane = jnp.stack(planes)
    shard = jnp.zeros((seqs,) + part.shape, part.dtype)
    mine = take(by_plane, (place.y - place.z_high) % seqs, 0)
    shard = lax.dynamic_update_index_in_dim(shard, mine, place.z_high, 0)
    for k in range(1, seqs):
        pairs = []
        for z, x, c in place.everyone():
            high, low = divmod(z, place.z_low_size)
            other = ((high + k) % seqs) * place.z_low_size + low
            pairs.append((place.index(z, x, c), place.index(other, x, c)))
        sent = take(by_plane, (place.y - place.z_high - k) % seqs, 0)
        got = lax.ppermute(sent, "fsdp", pairs)
        shard = lax.dynamic_update_index_in_dim(shard, got, (place.z_high - k) % seqs, 0)
    return shard.reshape(-1, part.shape[1]).astype(F32)


def sum_over(axis, count, value):
    bit = 1
    while bit < count:
        value = value + lax.ppermute(value, axis, [(i, i ^ bit) for i in range(count)])
        bit *= 2
    return value


def head_window(head):
    low = head * HEAD_SIZE // 128 * 128
    high = -(-(head + 1) * HEAD_SIZE // 128) * 128
    return low, high


def sigmoid(value):
    return 1.0 / (1.0 + jnp.exp(-value))


def conv_parts(values, taps_ref, seg_col):
    rows = values.shape[0]
    index = lax.broadcasted_iota(jnp.int32, (rows, 1), 0)
    near_one = (index >= 1) & (pltpu.roll(seg_col, 1, 0) == seg_col)
    near_two = (index >= 2) & (pltpu.roll(seg_col, 2, 0) == seg_col)
    prev_one = jnp.where(near_one, pltpu.roll(values, 1, 0), 0.0)
    prev_two = jnp.where(near_two, pltpu.roll(values, 2, 0), 0.0)
    conv = taps_ref[0:1] * values + taps_ref[1:2] * prev_one + taps_ref[2:3] * prev_two
    return conv, prev_one, prev_two, near_one, near_two


def masks(rows, seg_col, seg_row):
    at = lax.broadcasted_iota(jnp.int32, (rows, rows), 0)
    of = lax.broadcasted_iota(jnp.int32, (rows, rows), 1)
    return (seg_col == seg_row) & (at >= of)


def lanes_between(low, high, start, stop):
    lane = low + lax.broadcasted_iota(jnp.int32, (1, high - low), 1)
    return (lane >= start) & (lane < stop)


def relative(y_ref, seqs, piece):
    return lax.rem(y_ref[0] - piece + seqs, seqs)


def read_pieces(y_ref, ref):
    seqs = ref.shape[0]
    return jnp.concatenate([ref[relative(y_ref, seqs, s), 0] for s in range(seqs)], axis=0)


def write_pieces(y_ref, ref, value, low, high):
    seqs, rows = ref.shape[0], ref.shape[2]
    for s in range(seqs):
        ref[relative(y_ref, seqs, s), 0, :, low:high] = value[s * rows : (s + 1) * rows]


def mix_kernel(heads, y_ref, qkv_in, taps_ref, segc_ref, segr_ref, mixed_ref, qkv_ref, att_ref):
    qkv_ref[...] = read_pieces(y_ref, qkv_in)
    rows = qkv_ref.shape[0]
    qk_width = heads * FEAT
    width = heads * HEAD_SIZE
    seg_col = segc_ref[0]
    allowed = masks(rows, seg_col, segr_ref[0])
    queries = qkv_ref[:, 0:qk_width]
    keys = qkv_ref[:, qk_width : 2 * qk_width]
    for head in range(heads):
        mine = lanes_between(0, qk_width, head * FEAT, (head + 1) * FEAT)
        query = jnp.where(mine, queries, jnp.zeros_like(queries))
        scores = dot(query, keys, ((1,), (1,))) * 0.25
        kern = jnp.where(allowed, 1.0 + scores + 0.5 * scores * scores, 0.0)
        den = jnp.sum(kern, axis=1, keepdims=True)
        low, high = head_window(head)
        high = min(high, width)
        num = dot(kern.astype(BF16), qkv_ref[:, 2 * qk_width + low : 2 * qk_width + high])
        here = lanes_between(low, high, head * HEAD_SIZE, (head + 1) * HEAD_SIZE)
        att_ref[:, low:high] = jnp.where(here, num * (1.0 / den), att_ref[:, low:high])
    values = qkv_ref[:, 2 * qk_width : 2 * qk_width + width].astype(F32)
    conv = conv_parts(values, taps_ref, seg_col)[0]
    mixed = (att_ref[...] * conv * sigmoid(conv)).astype(BF16)
    write_pieces(y_ref, mixed_ref, mixed, 0, width)


def mix_back_kernel(
    heads, y_ref, qkv_in, dmixed_in, taps_ref, segc_ref, segr_ref, dqkv_ref, dtaps_ref,
    qkv_ref, dmixed_ref, att_ref, silu_ref, dv_ref,
):
    qkv_ref[...] = read_pieces(y_ref, qkv_in)
    dmixed_ref[...] = read_pieces(y_ref, dmixed_in).astype(F32)
    rows = qkv_ref.shape[0]
    qk_width = heads * FEAT
    width = heads * HEAD_SIZE
    seg_col = segc_ref[0]
    allowed = masks(rows, seg_col, segr_ref[0])
    queries = qkv_ref[:, 0:qk_width]
    keys = qkv_ref[:, qk_width : 2 * qk_width]
    values = qkv_ref[:, 2 * qk_width : 2 * qk_width + width].astype(F32)
    conv, prev_one, prev_two, near_one, near_two = conv_parts(values, taps_ref, seg_col)
    sig = sigmoid(conv)
    silu_ref[...] = dmixed_ref[...] * conv * sig
    dv_ref[...] = jnp.zeros_like(dv_ref)
    dq = jnp.zeros((rows, qk_width), F32)
    dk = jnp.zeros((rows, qk_width), F32)
    for head in range(heads):
        mine = lanes_between(0, qk_width, head * FEAT, (head + 1) * FEAT)
        query = jnp.where(mine, queries, jnp.zeros_like(queries))
        scores = dot(query, keys, ((1,), (1,))) * 0.25
        kern = jnp.where(allowed, 1.0 + scores + 0.5 * scores * scores, 0.0)
        inv_den = 1.0 / jnp.sum(kern, axis=1, keepdims=True)
        kern_low = kern.astype(BF16)
        low, high = head_window(head)
        high = min(high, width)
        value = qkv_ref[:, 2 * qk_width + low : 2 * qk_width + high]
        att = dot(kern_low, value) * inv_den
        here = lanes_between(low, high, head * HEAD_SIZE, (head + 1) * HEAD_SIZE)
        att_ref[:, low:high] = jnp.where(here, att, att_ref[:, low:high])
        datt = jnp.where(here, silu_ref[:, low:high], 0.0) * inv_den
        row_dot = jnp.sum(datt * att, axis=1, keepdims=True)
        datt_low = datt.astype(BF16)
        dkern = dot(datt_low, value, ((1,), (1,))) - row_dot
        dscores = jnp.where(allowed, dkern * (0.25 + 0.25 * scores), 0.0).astype(BF16)
        dq = dq + jnp.where(mine, dot(dscores, keys), 0.0)
        dk = dk + dot(dscores, query, ((0,), (0,)))
        dv_ref[:, low:high] += dot(kern_low, datt_low, ((0,), (0,)))
    dconv = dmixed_ref[...] * att_ref[...] * sig * (1.0 + conv * (1.0 - sig))
    dtaps_ref[0, 0:1] = jnp.sum(dconv * values, axis=0, keepdims=True)
    dtaps_ref[0, 1:2] = jnp.sum(dconv * prev_one, axis=0, keepdims=True)
    dtaps_ref[0, 2:3] = jnp.sum(dconv * prev_two, axis=0, keepdims=True)
    dtaps_ref[0, 3:8] = jnp.zeros((5, width), F32)
    back_one = pltpu.roll(jnp.where(near_one, dconv, 0.0), rows - 1, 0)
    back_two = pltpu.roll(jnp.where(near_two, dconv, 0.0), rows - 2, 0)
    dv = (
        dv_ref[...]
        + taps_ref[0:1] * dconv
        + taps_ref[1:2] * back_one
        + taps_ref[2:3] * back_two
    )
    write_pieces(y_ref, dqkv_ref, dq.astype(BF16), 0, qk_width)
    write_pieces(y_ref, dqkv_ref, dk.astype(BF16), qk_width, 2 * qk_width)
    write_pieces(y_ref, dqkv_ref, dv.astype(BF16), 2 * qk_width, 2 * qk_width + width)
    write_pieces(y_ref, dqkv_ref, jnp.zeros((rows, SMALL), BF16), 2 * qk_width + width, None)


def seg_specs(rows):
    return [
        pl.BlockSpec((1, rows, 1), lambda m: (m, 0, 0)),
        pl.BlockSpec((1, 1, rows), lambda m: (m, 0, 0)),
    ]


def piece_spec(shape):
    seqs, _, rows, width = shape
    return pl.BlockSpec((seqs, 1, rows, width), lambda m: (0, m, 0, 0))


def mix_forward(heads, y, qkv, taps, segments):
    seqs, micro, rows, qkv_width = qkv.shape
    group = seqs * rows
    width = heads * HEAD_SIZE
    return pl.pallas_call(
        partial(mix_kernel, heads),
        grid=(micro,),
        out_shape=jax.ShapeDtypeStruct((seqs, micro, rows, width), BF16),
        in_specs=[
            pl.BlockSpec(memory_space=pltpu.SMEM),
            piece_spec(qkv.shape),
            pl.BlockSpec(taps.shape, lambda m: (0, 0)),
            *seg_specs(group),
        ],
        out_specs=piece_spec((seqs, micro, rows, width)),
        scratch_shapes=[pltpu.VMEM((group, qkv_width), BF16), pltpu.VMEM((group, width), F32)],
        compiler_params=pltpu.CompilerParams(vmem_limit_bytes=48 * 2**20),
    )(y.reshape(1), qkv, taps, segments[:, :, None], segments[:, None, :])


def mix_backward(heads, y, qkv, dmixed, taps, segments):
    seqs, micro, rows, qkv_width = qkv.shape
    group = seqs * rows
    width = heads * HEAD_SIZE
    return pl.pallas_call(
        partial(mix_back_kernel, heads),
        grid=(micro,),
        out_shape=(
            jax.ShapeDtypeStruct(qkv.shape, BF16),
            jax.ShapeDtypeStruct((micro, 8, width), F32),
        ),
        in_specs=[
            pl.BlockSpec(memory_space=pltpu.SMEM),
            piece_spec(qkv.shape),
            piece_spec(dmixed.shape),
            pl.BlockSpec(taps.shape, lambda m: (0, 0)),
            *seg_specs(group),
        ],
        out_specs=(
            piece_spec(qkv.shape),
            pl.BlockSpec((1, 8, width), lambda m: (m, 0, 0)),
        ),
        scratch_shapes=[pltpu.VMEM((group, qkv_width), BF16)]
        + [pltpu.VMEM((group, width), F32)] * 4,
        compiler_params=pltpu.CompilerParams(vmem_limit_bytes=56 * 2**20),
    )(y.reshape(1), qkv, dmixed, taps, segments[:, :, None], segments[:, None, :])


def copy_kernel(source_ref, out_ref):
    out_ref[...] = source_ref[...]


def take_tiles(whole, part, parts, order):
    shards, tiles = whole.shape[0], whole.shape[1] // parts
    return pl.pallas_call(
        copy_kernel,
        grid=(shards,),
        out_shape=jax.ShapeDtypeStruct((shards, tiles, 8, 128), whole.dtype),
        in_specs=[pl.BlockSpec((1, tiles, 8, 128), lambda i: (order(i), part, 0, 0))],
        out_specs=pl.BlockSpec((1, tiles, 8, 128), lambda i: (i, 0, 0, 0)),
        compiler_params=pltpu.CompilerParams(vmem_limit_bytes=48 * 2**20),
    )(whole)


def up_kernel(rows_ref, tiles_ref, gate_ref, up_ref, hidden_ref):
    count = tiles_ref.shape[2]
    depth = rows_ref.shape[1]
    weight = jnp.concatenate(
        [tiles_ref[:, :, i].reshape(depth, 128) for i in range(count)], axis=1
    )
    up = dot(rows_ref[...], weight)
    gate = gate_ref[...]
    up_ref[...] = up
    hidden_ref[...] = (gate * sigmoid(gate) * up).astype(BF16)


def up_hidden(rows, whole, shape, gate, count=5):
    row_tiles, columns = shape[0] // 8, shape[1]
    tiles = whole.reshape(whole.shape[0], 2 * row_tiles, columns // 128, 8, 128)
    block = (whole.shape[0], row_tiles, count, 8, 128)
    wide = pl.BlockSpec((rows.shape[0], count * 128), lambda j: (0, j))
    return pl.pallas_call(
        up_kernel,
        grid=(-(-columns // (count * 128)),),
        out_shape=(
            jax.ShapeDtypeStruct((rows.shape[0], columns), F32),
            jax.ShapeDtypeStruct((rows.shape[0], columns), BF16),
        ),
        in_specs=[
            pl.BlockSpec(rows.shape, lambda j: (0, 0)),
            pl.BlockSpec(block, lambda j: (0, 0, j, 0, 0)),
            wide,
        ],
        out_specs=(wide, wide),
        compiler_params=pltpu.CompilerParams(vmem_limit_bytes=48 * 2**20),
    )(rows, tiles, gate)


class Gather:
    def __init__(self, arrays):
        self.shapes = [a.shape for a in arrays]
        self.joined = not any(a.shape[0] % 8 or a.shape[1] % 128 for a in arrays)
        if not self.joined:
            self.raw = [lax.all_gather(a, "fsdp", axis=0, tiled=True) for a in arrays]
            return
        counts = [a.size // 1024 for a in arrays]
        buffer = jnp.zeros((max(GATHER_TILES, sum(counts)), 8, 128), arrays[0].dtype)
        at = 0
        for a, count in zip(arrays, counts):
            t = a.reshape(a.shape[0] // 8, 8, a.shape[1] // 128, 128)
            t = jnp.swapaxes(t, 1, 2).reshape(-1, 8, 128)
            buffer = lax.dynamic_update_slice(buffer, t, (at, 0, 0))
            at += count
        self.raw = [lax.all_gather(buffer, "fsdp", axis=0, tiled=False)]

    def after(self, *values):
        count = len(self.raw)
        values = fence(*self.raw, *values)
        self.raw = list(values[:count])
        return values[count:]

    def arrays(self):
        if not self.joined:
            return self.raw
        gathered = []
        at = 0
        for rows, columns in self.shapes:
            count = rows * columns // 1024
            t = self.raw[0][:, at : at + count]
            t = t.reshape(-1, rows // 8, columns // 128, 8, 128)
            gathered.append(jnp.swapaxes(t, 2, 3).reshape(-1, columns))
            at += count
        return gathered


def on_device(
    tokens,
    seq_order,
    seq_lengths,
    valid_count,
    teacher,
    norm_one,
    w_query,
    w_key,
    w_value,
    conv_taps,
    w_out,
    norm_two,
    w_gate,
    w_up,
    w_down,
):
    place = Place()
    seqs, y = place.seqs, place.y
    micro, rows_dev, model = tokens.shape[0], tokens.shape[2], tokens.shape[3]
    group = seqs * rows_dev
    own_rows = micro * rows_dev
    heads = HEADS // seqs
    qk_width = heads * FEAT
    width = heads * HEAD_SIZE
    slots = micro * place.fsdp * group
    bits = place.fsdp.bit_length() - 1
    seq_bits = seqs.bit_length() - 1

    def columns(weight):
        part = weight.shape[1] // seqs
        return lax.dynamic_slice_in_dim(weight, y * part, part, 1)

    shard_rows = w_query.shape[0]
    valid = valid_count[:, 0]
    coded = jnp.stack([valid // 16, valid % 16], axis=1).reshape(1, 2 * micro).astype(BF16)
    first_row = lax.broadcasted_iota(jnp.int32, (shard_rows, 2 * micro), 0) == 0
    small = jnp.concatenate(
        [
            norm_one[:, None],
            norm_two[:, None],
            conv_taps.T,
            jnp.where(first_row, coded, jnp.zeros_like(coded)),
        ],
        axis=1,
    )
    small = jnp.pad(small, ((0, 0), (0, SMALL - small.shape[1])))
    first_shard = jnp.concatenate(
        [columns(w_query), columns(w_key), columns(w_value), small], axis=1
    )
    out_part = spread_rows(place, w_out)
    first, gate_w, out_w = Gather([first_shard, columns(w_gate), out_part]).arrays()
    down_part = spread_rows(place, w_down)
    late = Gather([columns(w_up), down_part])
    out_w = plane_rows(place, out_w)

    qkv_width = 2 * qk_width + width
    wide = qkv_width + SMALL
    small_all = first[:, qkv_width : qkv_width + 16].astype(F32).T
    gain_one, gain_two = small_all[0], small_all[1]
    taps = lax.dynamic_slice_in_dim(small_all[2:5], y * width, width, 1)
    taps = jnp.pad(taps, ((0, 5), (0, 0)))
    coded_sum = jnp.sum(small_all[5 : 5 + 2 * micro], axis=1)
    total = 16.0 * jnp.sum(coded_sum[0::2]) + jnp.sum(coded_sum[1::2])
    scale = slots / total

    order = seq_order[:, 0, 0]
    local = jnp.arange(rows_dev, dtype=jnp.int32)
    order_k = gather_seq(place, order)
    tokens_k = gather_seq(place, tokens[:, 0])
    picks = [(o[..., None] == local).astype(BF16) for o in order_k]
    pick = picks[0]
    packed_k = [
        jnp.einsum("mij,mjd->mid", o, t, preferred_element_type=BF16).reshape(own_rows, model)
        for o, t in zip(picks, tokens_k)
    ]
    wanted = jnp.einsum("mij,mjd->mid", pick, teacher[:, 0], preferred_element_type=BF16)
    wanted = wanted.reshape(own_rows, model)
    keep = (order + y * rows_dev < valid[:, None]).astype(F32).reshape(own_rows, 1)
    ends = jnp.cumsum(seq_lengths[:, 0], axis=1)
    positions = jnp.arange(group, dtype=jnp.int32)
    segments = jnp.sum((positions[None, :, None] >= ends[:, None, :]).astype(jnp.int32), axis=2)

    packed = jnp.concatenate(packed_k, axis=0)
    packed_f = packed.astype(F32)
    root_one = lax.rsqrt(jnp.mean(packed_f * packed_f, axis=1, keepdims=True) + EPSILON)
    n_one = (packed_f * root_one * gain_one).astype(BF16)
    qkv = dot(n_one, first).astype(BF16).reshape(seqs, micro, rows_dev, wide)
    mixed = mix_forward(heads, y, qkv, taps, segments).reshape(seqs * own_rows, width)

    def pieces(value):
        return [value[k * own_rows : (k + 1) * own_rows] for k in range(seqs)]

    def scatter(parts):
        got = [seq_send(place, parts[k].astype(BF16), seqs - k) for k in range(1, seqs)]
        return parts[0], got

    def project(rows_k, weight, dims=((1,), (0,))):
        parts = [None] * seqs
        for k in list(range(1, seqs)) + [0]:
            parts[k] = dot(rows_k[k], weight, dims)
        return parts

    packed_own = packed_k[0].astype(F32)
    own, got = scatter(project(pieces(mixed), out_w))
    own, *got = fence(own, *got)
    resid = packed_own + own
    for part in got:
        resid = resid + part.astype(F32)
    root_two = lax.rsqrt(jnp.mean(resid * resid, axis=1, keepdims=True) + EPSILON)
    n_two_k = gather_seq(place, (resid * root_two * gain_two).astype(BF16))
    gate_k = [dot(n, gate_w) for n in n_two_k]
    gate_k = list(late.after(*gate_k))
    whole = late.raw[0]
    direct = late.joined and whole.shape[1] == 2 * late.shapes[0][0] * late.shapes[0][1] // 1024
    up_k, hidden_k = [None] * seqs, [None] * seqs
    if direct:
        for k in list(range(1, seqs)) + [0]:
            up_k[k], hidden_k[k] = up_hidden(n_two_k[k], whole, late.shapes[0], gate_k[k])
        per = place.fsdp // seqs
        tiles = take_tiles(whole, 1, 2, lambda i: (i % seqs) * per + i // seqs)
        rows_down, columns_down = late.shapes[1]
        tiles = tiles.reshape(-1, rows_down // 8, columns_down // 128, 8, 128)
        down_w = jnp.swapaxes(tiles, 2, 3).reshape(-1, columns_down)
    else:
        up_w, down_w = late.arrays()
        down_w = plane_rows(place, down_w)
        for k in range(seqs):
            up_k[k] = dot(n_two_k[k], up_w)
            hidden_k[k] = (gate_k[k] * jax.nn.sigmoid(gate_k[k]) * up_k[k]).astype(BF16)
    sig_k = [jax.nn.sigmoid(g) for g in gate_k]
    own, got = scatter(project(hidden_k, down_w))
    if direct:
        late.raw[0], own = fence(late.raw[0], own)
        up_w, _ = late.arrays()
    own, up_w, *got = fence(own, up_w, *got)
    result = resid + own
    for part in got:
        result = result + part.astype(F32)
    error = (result - wanted.astype(F32)) * keep
    d_result = scale * error
    d_low = d_result.astype(BF16)
    d_low_k = gather_seq(place, d_low)
    squares = sum_over("fsdp", place.fsdp, jnp.sum(error * error, axis=(0, 1), keepdims=True))

    def to_given(value):
        value = value.astype(BF16).reshape(micro, rows_dev, model)
        return jnp.einsum("mij,mid->mjd", pick, value, preferred_element_type=BF16)

    output = to_given(result)

    def ffn_back(k, d_low):
        d_hidden = dot(d_low, down_w, ((1,), (1,)))
        gate, up, sig = gate_k[k], up_k[k], sig_k[k]
        d_gate = (d_hidden * up * sig * (1.0 + gate * (1.0 - sig))).astype(BF16)
        d_up = (d_hidden * gate * sig).astype(BF16)
        return d_gate, d_up

    column_labels = list(range(bits - 1, -1, -1))
    row_labels = list(range(bits - 1 - seq_bits, -1, -1)) + list(
        range(bits - 1, bits - 1 - seq_bits, -1)
    )
    x_bits = list(range(1, bits - 2))
    x_first = [[0], x_bits, [bits - 2], [bits - 1]]

    def by_rows(grad, order):
        view = grad.reshape([2] * bits + [grad.shape[0] // place.fsdp, grad.shape[1]])
        return Reduction(place, view, row_labels, order)

    def by_columns(grad, order):
        view = grad.reshape([2] * bits + [grad.shape[0] // place.fsdp, grad.shape[1]])
        return Reduction(place, view, column_labels, order)

    def weight_grad(left, right):
        return dot(left, right, ((0,), (0,))).astype(BF16)

    d_gate_own, d_up_own = ffn_back(0, d_low)
    hidden = jnp.concatenate(hidden_k, axis=0)
    n_two = jnp.concatenate(n_two_k, axis=0)
    d_gate_own, d_up_own, squares, *d_low_others = fence(
        d_gate_own, d_up_own, squares, *d_low_k[1:]
    )
    down = by_rows(weight_grad(hidden, jnp.concatenate([d_low, *d_low_others])), x_first)
    d_low_others = down.start(*d_low_others)
    d_pairs = [(d_gate_own, d_up_own)] + [
        ffn_back(k + 1, d) for k, d in enumerate(d_low_others)
    ]
    d_gate_k = [a for a, b in d_pairs]
    d_up_k = [b for a, b in d_pairs]
    d_gate = jnp.concatenate(d_gate_k, axis=0)
    d_up = jnp.concatenate(d_up_k, axis=0)
    gate_grad = weight_grad(n_two, d_gate)
    gate_grad, d_up, *d_both = fence(gate_grad, d_up, *d_gate_k, *d_up_k)
    gate_sum = lax.psum_scatter(gate_grad, "fsdp", scatter_dimension=0, tiled=True)
    d_both = down.after(*d_both)
    d_both = down.start(*d_both)
    d_gate_k, d_up_k = d_both[:seqs], d_both[seqs:]

    def ffn_part(k):
        return dot(d_gate_k[k], gate_w, ((1,), (1,))) + dot(d_up_k[k], up_w, ((1,), (1,)))

    parts = [ffn_part(k).astype(BF16) for k in range(1, seqs)]
    d_both = place.in_turn(*parts, d_up, *d_gate_k, *d_up_k)
    parts, d_up = d_both[: seqs - 1], d_both[seqs - 1]
    d_gate_k, d_up_k = d_both[seqs:-seqs], d_both[-seqs:]
    got = [seq_send(place, part, seqs - 1 - k) for k, part in enumerate(parts)]
    up = by_columns(weight_grad(n_two, d_up), x_first)
    d_gate_k[0], d_up_k[0] = up.start(d_gate_k[0], d_up_k[0])
    own = ffn_part(0)
    own, = up.after(own)
    own, *got = place.in_turn(own, *got)
    d_n_two = own
    for part in got:
        d_n_two = d_n_two + part.astype(F32)
    grad_norm_two = jnp.sum(d_n_two * resid * root_two, axis=0)
    d_scaled = d_n_two * gain_two
    d_resid = (
        d_result
        + root_two * d_scaled
        - resid * root_two**3 * jnp.mean(d_scaled * resid, axis=1, keepdims=True)
    )
    dm_own, = place.in_turn(d_resid.astype(BF16))
    dm_k = gather_seq(place, dm_own)
    dm_own, = up.start(dm_own)
    d_mixed_own = dot(dm_own, out_w, ((1,), (1,)))
    d_mixed_own, *dm_others = place.in_turn(d_mixed_own, *dm_k[1:])
    out = by_rows(weight_grad(mixed, jnp.concatenate([dm_own, *dm_others])), x_first)
    dm_others = out.start(*dm_others)
    d_mixed = jnp.concatenate(
        [d_mixed_own] + [dot(d, out_w, ((1,), (1,))) for d in dm_others]
    ).reshape(seqs, micro, rows_dev, width)
    d_mixed, = down.after(d_mixed)
    d_mixed, = down.start(d_mixed)
    d_mixed, = out.after(d_mixed)
    d_mixed, = out.start(d_mixed)
    d_qkv, d_taps = mix_backward(heads, y, qkv, d_mixed, taps, segments)
    d_qkv = d_qkv.reshape(seqs * own_rows, wide)
    d_taps = jnp.sum(d_taps, axis=0)[:3]
    others = [dot(d, first, ((1,), (1,))) for d in pieces(d_qkv)[1:]]
    sent = [part.astype(BF16) for part in others]
    *sent, d_qkv = place.in_turn(*sent, d_qkv)
    got = [seq_send(place, part, seqs - 1 - k) for k, part in enumerate(sent)]
    own = dot(d_qkv[:own_rows], first, ((1,), (1,)))
    grad_norm_one = sum(
        jnp.sum(part * (p.astype(F32) * r), axis=0)
        for part, p, r in zip([own, *others], packed_k, pieces(root_one))
    )
    d_taps_wide = lax.dynamic_update_slice_in_dim(
        jnp.zeros((3, model), F32), d_taps, y * width, 1
    )
    extra = jnp.concatenate(
        [grad_norm_one[None], grad_norm_two[None], d_taps_wide, jnp.zeros((3, model), F32)]
    )
    extra = jnp.pad(extra.T, ((0, 0), (qkv_width, SMALL - extra.shape[0])))
    grad_first = (dot(n_one, d_qkv, ((0,), (0,))) + extra).astype(BF16)
    grad_first, own = fence(grad_first, own)
    first_sum = lax.psum_scatter(grad_first, "fsdp", scatter_dimension=0, tiled=True)
    own, *got = place.in_turn(own, *got)

    d_n_one = own
    for part in got:
        d_n_one = d_n_one + part.astype(F32)
    root_own = root_one[:own_rows]
    d_scaled = d_n_one * gain_one
    d_packed = (
        d_resid
        + root_own * d_scaled
        - packed_own * root_own**3 * jnp.mean(d_scaled * packed_own, axis=1, keepdims=True)
    )
    def join(parts):
        return jnp.concatenate(parts, axis=1).astype(F32)

    d_packed, = up.after(d_packed)
    d_packed, = up.start(d_packed)
    d_packed, gate_sum = place.in_turn(d_packed, gate_sum)
    squares, d_packed = place.in_turn(squares, d_packed)
    squares = sum_over("seq", seqs, squares)
    squares, gate_sum = place.in_turn(squares, gate_sum)
    gate_k = gather_seq(place, gate_sum)
    input_grad = to_given(d_packed)
    down.after()
    down.start()
    out.after()
    out.start()
    up.after()
    up.start()
    down.after()
    down_k = unspread_start(place, down.result())
    gate_k = place.in_turn(*gate_k)
    grad_gate = join(in_order(place, gate_k))
    out.after()
    out.start()
    down_k = place.in_turn(*down_k)
    grad_down = unspread_end(place, down_k)
    up.after()
    up_k = gather_seq(place, up.result())
    out.after()
    out_k = unspread_start(place, out.result())
    first_sum, = place.in_turn(first_sum)
    first_k = gather_seq(place, first_sum)
    out_k = place.in_turn(*out_k)
    grad_out = unspread_end(place, out_k)
    up_k = place.in_turn(*up_k)
    grad_up = join(in_order(place, up_k))
    first_parts = in_order(place, first_k)
    loss = (squares[0, 0] + place.turn[0, 0]) / (total * model)
    extra_sum = sum(part[:, qkv_width:].astype(F32) for part in first_parts)
    return (
        output[:, None],
        input_grad[:, None],
        extra_sum[:, 0],
        join([part[:, :qk_width] for part in first_parts]),
        join([part[:, qk_width : 2 * qk_width] for part in first_parts]),
        join([part[:, 2 * qk_width : qkv_width] for part in first_parts]),
        extra_sum[:, 2:5].T,
        grad_out,
        extra_sum[:, 1],
        grad_gate,
        grad_up,
        grad_down,
        loss,
    )


def solution(mesh):
    rows = P(None, "fsdp", "seq", None)
    placed = (
        rows,
        rows,
        P(None, "fsdp", None),
        P(None, "fsdp"),
        rows,
        P("fsdp"),
        P("fsdp", None),
        P("fsdp", None),
        P("fsdp", None),
        P(None, "fsdp"),
        P("fsdp", None),
        P("fsdp"),
        P("fsdp", None),
        P("fsdp", None),
        P("fsdp", None),
    )
    return jax.shard_map(
        on_device,
        mesh=mesh,
        in_specs=placed,
        out_specs=(
            rows,
            rows,
            P("fsdp"),
            P("fsdp", None),
            P("fsdp", None),
            P("fsdp", None),
            P(None, "fsdp"),
            P("fsdp", None),
            P("fsdp"),
            P("fsdp", None),
            P("fsdp", None),
            P("fsdp", None),
            P(),
        ),
        check_vma=False,
    )
```
